128 devices in a mesh: sweep: 8 (over z, core), layer: 16 (over x, y).
Axes of the slice: x: 4, y: 4, z: 4, core: 2. Of those that a mesh axis runs over, the one named last changes fastest.
Arguments:
- green: bfloat16 [8, 2, 8192, 8192], P('sweep', None, 'layer'), may hold values from -1 to 1
- down_source: float32 [8, 2, 16, 8192], P('sweep', None, None, 'layer'), may hold values from -6 to 6
- up_source: float32 [8, 2, 16, 8192], P('sweep', None, None, 'layer'), may hold values from -6 to 6
Outputs:
- total: float32 [8, 2, 16, 8192], P('sweep', None, None, 'layer')
The draws below stay inside these ranges and needn't reach their ends.
All inputs are finite; a program needn't handle non-finite values.
Results may differ from the reference program's by a relative error of at most 0.02.
Values may be sent and summed in bfloat16 or wider, within the bound.
No kernel may reach another device: no remote copies, remote signals or barrier semaphores. Data moves between devices by JAX's collectives and lax.ppermute only.
A program may use at most 64 MiB of HBM per device.

```python
import math
import jax
import jax.numpy as jnp
from jax import lax

W = 8192
SOURCES = 16
LAYERS = 8


def draw_green(key, part):
    base_key = jax.random.fold_in(key, 7)
    spread = 0.5 / math.sqrt(2.0 * W)

    def draw_layer(layer_index):
        layer_key = jax.random.fold_in(base_key, layer_index)
        key_offdiag, key_modulus, key_angles = jax.random.split(layer_key, 3)
        offdiag = jax.random.normal(key_offdiag, (2, W, W), jnp.float32) * spread
        modulus = jax.random.uniform(key_modulus, (W,), jnp.float32, 0.6, 0.9)
        angles = jax.random.uniform(key_angles, (W,), jnp.float32, -jnp.pi, jnp.pi)
        diagonal = jnp.stack([modulus * jnp.cos(angles), modulus * jnp.sin(angles)])
        row_ids = lax.broadcasted_iota(jnp.int32, (W, W), 0)
        col_ids = lax.broadcasted_iota(jnp.int32, (W, W), 1)
        on_diagonal = jnp.where(row_ids == col_ids, 1.0, 0.0).astype(jnp.float32)
        matrix = offdiag + on_diagonal[None] * diagonal[:, :, None]
        matrix = jnp.clip(matrix, -1.0, 1.0)
        return matrix.astype(jnp.bfloat16)
    return lax.map(draw_layer, jnp.arange(LAYERS, dtype=jnp.int32))


def steps_of(own_key, shape, cuts, least, high):
    level, own = 1.0, jax.random.fold_in(own_key, 6)
    for axis_at, shards_of in cuts:
        heights = jnp.exp(jax.random.uniform(jax.random.fold_in(own, axis_at), (shards_of,), jnp.float32, least / len(cuts), high / len(cuts)))
        level = level * jnp.repeat(heights, shape[axis_at] // shards_of).reshape([-1 if axis == axis_at else 1 for axis in range(len(shape))])
    return level


def bell_draw(stream_key, shape, deviation, reach, cuts=(), held_as=jnp.bfloat16):
    factor_of = steps_of(stream_key, shape, cuts, -0.22, 0.18) if cuts else 1.0
    array = jax.random.normal(stream_key, shape, jnp.float32) * deviation * factor_of
    return jnp.minimum(jnp.maximum(array, -reach), reach).astype(held_as)


def setup_inputs(seed: int = 0) -> dict:
    streams_of = jax.random.split(jax.random.key(seed), 4)
    green = draw_green(jax.random.fold_in(streams_of[3], 71), 0)
    down_source = bell_draw(streams_of[1], (LAYERS, 2, SOURCES, W), 1.0, 6.0, ((0, 8), (3, 16)), jnp.float32)
    up_source = bell_draw(streams_of[2], (LAYERS, 2, SOURCES, W), 1.0, 6.0, ((0, 8), (3, 16)), jnp.float32)
    return {"green": green, "down_source": down_source, "up_source": up_source}


def rows_product(trace_in, matrix):
    contract = (((1,), (1,)), ((), ()))
    real_real = lax.dot_general(trace_in[0], matrix[0], contract, preferred_element_type=jnp.float32)
    imag_imag = lax.dot_general(trace_in[1], matrix[1], contract, preferred_element_type=jnp.float32)
    real_imag = lax.dot_general(trace_in[0], matrix[1], contract, preferred_element_type=jnp.float32)
    imag_real = lax.dot_general(trace_in[1], matrix[0], contract, preferred_element_type=jnp.float32)
    return jnp.stack([real_real - imag_imag, real_imag + imag_real])


def cols_product(trace_in, matrix):
    real_real = jnp.dot(trace_in[0], matrix[0], preferred_element_type=jnp.float32)
    imag_imag = jnp.dot(trace_in[1], matrix[1], preferred_element_type=jnp.float32)
    real_imag = jnp.dot(trace_in[0], matrix[1], preferred_element_type=jnp.float32)
    imag_real = jnp.dot(trace_in[1], matrix[0], preferred_element_type=jnp.float32)
    return jnp.stack([real_real - imag_imag, real_imag + imag_real])


def reference(green, down_source, up_source):
    layers = green.shape[0]
    outgoing = jnp.zeros((2, SOURCES, W), jnp.bfloat16)
    down_list = []
    for layer_index in range(layers):
        down_row = down_source[layer_index] + rows_product(outgoing, green[layer_index])
        down_list.append(down_row)
        outgoing = down_row.astype(jnp.bfloat16)
    outgoing = jnp.zeros((2, SOURCES, W), jnp.bfloat16)
    total_list = [None] * layers
    for layer_index in reversed(range(layers)):
        total_row = (up_source[layer_index] + down_list[layer_index]) + cols_product(outgoing, green[layer_index])
        total_list[layer_index] = total_row
        outgoing = total_row.astype(jnp.bfloat16)
    return jnp.stack(total_list)
```

```python
import functools

import jax
import jax.numpy as jnp
from jax import lax
from jax.experimental import pallas as pl
from jax.experimental.pallas import tpu as pltpu
from jax.sharding import PartitionSpec as P

F32, BF16 = jnp.float32, jnp.bfloat16
MIB = 1 << 20


def pick_halves(matrix, half, chips):
    parts, rows, cols = matrix.shape
    wide = cols // (2 * chips)

    def body(half_ref, in_ref, out_ref):
        out_ref[...] = in_ref[...]

    return pl.pallas_call(
        body,
        grid_spec=pltpu.PrefetchScalarGridSpec(
            num_scalar_prefetch=1,
            grid=(chips,),
            in_specs=[pl.BlockSpec((parts, rows, wide), lambda i, h: (0, 0, 2 * i + h[0]))],
            out_specs=pl.BlockSpec((parts, rows, wide), lambda i, h: (0, 0, i)),
        ),
        out_shape=jax.ShapeDtypeStruct((parts, rows, cols // 2), BF16),
        compiler_params=pltpu.CompilerParams(vmem_limit_bytes=8 * MIB),
        name="pick_halves",
    )(half, matrix)


def load_half(use_own, half, matrix, received, chips):
    parts, rows, cols = matrix.shape
    wide = cols // (2 * chips)

    def body(own_ref, half_ref, matrix_ref, received_ref, out_ref, sems):
        @pl.when(own_ref[0] == 1)
        def _():
            start = half_ref[0] * wide

            def copy(i):
                at = pl.multiple_of(2 * i * wide + start, wide)
                return pltpu.make_async_copy(
                    matrix_ref.at[:, :, pl.ds(at, wide)],
                    out_ref.at[:, :, pl.ds(i * wide, wide)],
                    sems.at[i],
                )

            for i in range(chips):
                copy(i).start()
            for i in range(chips):
                copy(i).wait()

        @pl.when(own_ref[0] != 1)
        def _():
            def copy(i):
                return pltpu.make_async_copy(
                    received_ref.at[:, :, pl.ds(i * wide, wide)],
                    out_ref.at[:, :, pl.ds(i * wide, wide)],
                    sems.at[i],
                )

            for i in range(chips):
                copy(i).start()
            for i in range(chips):
                copy(i).wait()

    return pl.pallas_call(
        body,
        in_specs=[
            pl.BlockSpec(memory_space=pltpu.SMEM),
            pl.BlockSpec(memory_space=pltpu.SMEM),
            pl.BlockSpec(memory_space=pl.ANY),
            pl.BlockSpec(memory_space=pl.ANY),
        ],
        out_specs=pl.BlockSpec(memory_space=pltpu.VMEM),
        out_shape=pltpu.VMEM((parts, rows, cols // 2), BF16),
        scratch_shapes=[pltpu.SemaphoreType.DMA((chips,))],
        compiler_params=pltpu.CompilerParams(vmem_limit_bytes=20 * MIB),
        name="load_half",
    )(use_own, half, matrix, received)


def vmem_call(body, out_shape, name, flops):
    def call(*args):
        return pl.pallas_call(
            body,
            in_specs=[pl.BlockSpec(memory_space=pltpu.VMEM)] * len(args),
            out_specs=jax.tree.map(lambda _: pl.BlockSpec(memory_space=pltpu.VMEM), out_shape),
            out_shape=out_shape,
            compiler_params=pltpu.CompilerParams(vmem_limit_bytes=24 * MIB),
            cost_estimate=pl.CostEstimate(flops=flops, bytes_accessed=1 << 16, transcendentals=0),
            name=name,
        )(*args)

    return call


def down_body(x_ref, g_ref, core_ref, base_ref, mine_ref, theirs_ref):
    chips, rhs, wide = x_ref.shape
    contract = (((1,), (1,)), ((), ()))
    with_real = with_imag = None
    for i in range(chips):
        at = slice(i * wide, (i + 1) * wide)
        r = lax.dot_general(x_ref[i], g_ref[0, :, at], contract, preferred_element_type=F32)
        m = lax.dot_general(x_ref[i], g_ref[1, :, at], contract, preferred_element_type=F32)
        with_real = r if i == 0 else with_real + r
        with_imag = m if i == 0 else with_imag + m
    n = rhs // 2
    real = with_real[:n] - with_imag[n:]
    imag = with_imag[:n] + with_real[n:]
    first = jnp.concatenate([real[:, :wide], imag[:, :wide]], axis=0)
    second = jnp.concatenate([real[:, wide:], imag[:, wide:]], axis=0)
    on_first = core_ref[0:1, 0:1] == 0
    mine_ref[...] = jnp.where(on_first, first, second) + base_ref[...]
    theirs_ref[...] = jnp.where(on_first, second, first)


def up_body(x_ref, g_ref, out_ref):
    chips, rhs, wide = out_ref.shape
    n = rhs // 2
    x = x_ref[...]
    for i in range(chips):
        at = slice(i * wide, (i + 1) * wide)
        r = jnp.dot(x, g_ref[0, :, at], preferred_element_type=F32)
        m = jnp.dot(x, g_ref[1, :, at], preferred_element_type=F32)
        out_ref[i, :n] = (r[:n] - m[n:]).astype(BF16)
        out_ref[i, n:] = (m[:n] + r[n:]).astype(BF16)


def local(green, down_source, up_source):
    planes = lax.axis_size("sweep") // 2
    chips = lax.axis_size("layer")
    matrix = green[0]
    rows, cols = matrix.shape[1:]
    wide = rows // 2
    rhs = 2 * down_source.shape[2]
    me = lax.axis_index("sweep")
    core, plane = me % 2, me // 2

    swap_pairs = [(i, i ^ 1) for i in range(2 * planes)]

    def swap(x):
        return lax.ppermute(x, "sweep", swap_pairs)

    def hop(x, a, b):
        pairs = [p for c in range(2) for p in ((2 * a + c, 2 * b + c), (2 * b + c, 2 * a + c))]
        return lax.ppermute(x, "sweep", pairs)

    def exchange(blocks):
        return lax.all_to_all(blocks, "layer", 0, 0, tiled=True)

    one = lambda v: v.astype(jnp.int32).reshape(1)
    received = swap(pick_halves(matrix, one(1 - core), chips))

    def halves(source):
        full = source.reshape(rhs, rows)
        own = lax.dynamic_slice(full, (0, core * wide), (rhs, wide))
        other = swap(lax.dynamic_slice(full, (0, (1 - core) * wide), (rhs, wide)))
        first = core == 0
        return jnp.where(first, own, other), jnp.where(first, other, own)

    down_a, down_b = halves(down_source)
    base_a, base_b = down_a, down_b
    up_a, up_b = halves(up_source)

    matrix_b = load_half(one(core == 1), one(core), matrix, received, chips)
    matrix_a = load_half(one(core == 0), one(core), matrix, received, chips)
    core_tile = jnp.broadcast_to(core.astype(jnp.int32), (8, 128))

    flops = 8 * rhs * rows * cols // 2
    part = jax.ShapeDtypeStruct((rhs, wide), F32)
    down_call = vmem_call(down_body, (part, part), "down_product", flops)
    up_call = vmem_call(up_body, jax.ShapeDtypeStruct((chips, rhs, wide), BF16), "up_product", flops)

    def down_product(x, mat, base):
        blocks = exchange(jnp.broadcast_to(x.astype(BF16), (chips, rhs, wide)))
        mine, theirs = down_call(blocks, mat, core_tile, base)
        return mine + swap(theirs)

    def up_product(x, mat, base):
        x = x.astype(BF16)
        other = swap(x)
        first = core == 0
        full = jnp.concatenate([jnp.where(first, x, other), jnp.where(first, other, x)], axis=1)
        blocks = exchange(up_call(full, mat))
        return base + jnp.sum(blocks.astype(F32), axis=0)

    here = lambda p: plane == p
    x = base_a
    for p in range(planes):
        if p > 0:
            x = hop(x.astype(BF16), p - 1, p)
            x = down_product(x, matrix_a, base_a)
            down_a = jnp.where(here(p), x, down_a)
        x = down_product(x, matrix_b, base_b)
        down_b = jnp.where(here(p), x, down_b)

    base_a, base_b = up_a + down_a, up_b + down_b
    total_a, total_b = base_a, base_b
    x = base_b
    for p in reversed(range(planes)):
        if p < planes - 1:
            x = hop(x.astype(BF16), p + 1, p)
            x = up_product(x, matrix_b, base_b)
            total_b = jnp.where(here(p), x, total_b)
        x = up_product(x, matrix_a, base_a)
        total_a = jnp.where(here(p), x, total_a)

    first = core == 0
    keep = jnp.where(first, total_a, total_b)
    other = swap(jnp.where(first, total_b, total_a))
    out = jnp.concatenate([jnp.where(first, keep, other), jnp.where(first, other, keep)], axis=1)
    return out.reshape(1, 2, rhs // 2, rows)


def solution(mesh):
    in_specs = (
        P("sweep", None, "layer", None),
        P("sweep", None, None, "layer"),
        P("sweep", None, None, "layer"),
    )
    out_specs = P("sweep", None, None, "layer")
    return jax.shard_map(local, mesh=mesh, in_specs=in_specs, out_specs=out_specs, check_vma=False)
```

```python
import jax
import jax.numpy as jnp
from jax import lax
from jax.experimental import pallas as pl
from jax.experimental.pallas import tpu as pltpu
from jax.sharding import PartitionSpec as P

F32, BF16 = jnp.float32, jnp.bfloat16
MIB = 1 << 20
VMEM = pl.BlockSpec(memory_space=pltpu.VMEM)
HBM = pl.BlockSpec(memory_space=pltpu.HBM)
SMEM = pl.BlockSpec(memory_space=pltpu.SMEM)


def copy_all(copies):
    for copy in copies:
        copy.start()
    for copy in copies:
        copy.wait()


def second_halves(matrix, chips):
    parts, rows, cols = matrix.shape
    wide = cols // (2 * chips)

    def body(matrix_ref, out_ref, sems):
        copy_all(
            [
                pltpu.make_async_copy(
                    matrix_ref.at[:, :, pl.ds((2 * i + 1) * wide, wide)],
                    out_ref.at[:, :, pl.ds(i * wide, wide)],
                    sems.at[i],
                )
                for i in range(chips)
            ]
        )

    return pl.pallas_call(
        body,
        in_specs=[HBM],
        out_specs=HBM,
        out_shape=pltpu.HBM((parts, rows, cols // 2), BF16),
        scratch_shapes=[pltpu.SemaphoreType.DMA((chips,))],
        compiler_params=pltpu.CompilerParams(vmem_limit_bytes=56 * MIB),
        name="second_halves",
    )(matrix)


def load_half(core, on_core, matrix, received, after, chips):
    parts, rows, cols = matrix.shape
    wide = cols // (2 * chips)

    def body(core_ref, matrix_ref, received_ref, after_ref, out_ref, sems):
        @pl.when(core_ref[0] == on_core)
        def _():
            copy_all(
                [
                    pltpu.make_async_copy(
                        matrix_ref.at[:, :, pl.ds(2 * i * wide, wide)],
                        out_ref.at[:, :, pl.ds(i * wide, wide)],
                        sems.at[i],
                    )
                    for i in range(chips)
                ]
            )

        @pl.when(core_ref[0] != on_core)
        def _():
            copy_all(
                [
                    pltpu.make_async_copy(
                        received_ref.at[:, :, pl.ds(i * wide, wide)],
                        out_ref.at[:, :, pl.ds(i * wide, wide)],
                        sems.at[i],
                    )
                    for i in range(chips)
                ]
            )

    return pl.pallas_call(
        body,
        in_specs=[SMEM, HBM, HBM, VMEM],
        out_specs=VMEM,
        out_shape=pltpu.VMEM((parts, rows, cols // 2), BF16),
        scratch_shapes=[pltpu.SemaphoreType.DMA((chips,))],
        compiler_params=pltpu.CompilerParams(vmem_limit_bytes=40 * MIB),
        name="load_half",
    )(core, matrix, received, after)


def vmem_call(body, out_shape, name, flops):
    def call(*args):
        return pl.pallas_call(
            body,
            in_specs=[VMEM] * len(args),
            out_specs=jax.tree.map(lambda _: VMEM, out_shape),
            out_shape=out_shape,
            compiler_params=pltpu.CompilerParams(vmem_limit_bytes=8 * MIB),
            cost_estimate=pl.CostEstimate(flops=flops, bytes_accessed=1 << 16, transcendentals=0),
            name=name,
        )(*args)

    return call


def down_body(x_ref, g_ref, first_ref, base_ref, mine_ref, theirs_ref):
    chips, rhs, wide = x_ref.shape
    contract = (((1,), (1,)), ((), ()))
    with_real = with_imag = None
    for i in range(chips):
        at = slice(i * wide, (i + 1) * wide)
        r = lax.dot_general(x_ref[i], g_ref[0, :, at], contract, preferred_element_type=F32)
        m = lax.dot_general(x_ref[i], g_ref[1, :, at], contract, preferred_element_type=F32)
        with_real = r if i == 0 else with_real + r
        with_imag = m if i == 0 else with_imag + m
    n = rhs // 2
    real = with_real[:n] - with_imag[n:]
    imag = with_imag[:n] + with_real[n:]
    first = jnp.concatenate([real[:, :wide], imag[:, :wide]], axis=0)
    second = jnp.concatenate([real[:, wide:], imag[:, wide:]], axis=0)
    keeps_first = first_ref[0:1, 0:1] == 1
    mine_ref[...] = jnp.where(keeps_first, first, second) + base_ref[...]
    theirs_ref[...] = jnp.where(keeps_first, second, first)


def up_body(x_ref, g_ref, out_ref):
    chips, rhs, wide = out_ref.shape
    n = rhs // 2
    x = x_ref[...]
    for i in range(chips):
        at = slice(i * wide, (i + 1) * wide)
        r = jnp.dot(x, g_ref[0, :, at], preferred_element_type=F32)
        m = jnp.dot(x, g_ref[1, :, at], preferred_element_type=F32)
        out_ref[i, :n] = (r[:n] - m[n:]).astype(BF16)
        out_ref[i, n:] = (m[:n] + r[n:]).astype(BF16)


def make_masks(me, count, shape):
    def body(me_ref, out_ref):
        index = me_ref[0]
        for p in range(count):
            out_ref[p] = jnp.full(shape, jnp.where(index // 2 == p, 1, 0), jnp.int32)
        out_ref[count] = jnp.full(shape, jnp.where(index % 2 == 0, 1, 0), jnp.int32)

    return pl.pallas_call(
        body,
        in_specs=[SMEM],
        out_specs=VMEM,
        out_shape=pltpu.VMEM((count + 1, *shape), jnp.int32),
        name="make_masks",
    )(me)


def local(green, down_source, up_source):
    planes = lax.axis_size("sweep") // 2
    chips = lax.axis_size("layer")
    matrix = green[0]
    rows, cols = matrix.shape[1:]
    wide = rows // 2
    rhs = 2 * down_source.shape[2]
    me = lax.axis_index("sweep")
    masks = make_masks(me.astype(jnp.int32).reshape(1), planes, (rhs, wide))
    tile_0 = masks[planes, :8, :128]
    tile_1 = 1 - tile_0
    masks = [masks[p] == 1 for p in range(planes + 1)]
    on_0 = masks.pop()

    def swap(x):
        return lax.ppermute(x, "sweep", [(i, i ^ 1) for i in range(2 * planes)])

    def hop(x, a, b):
        pairs = [p for c in range(2) for p in ((2 * a + c, 2 * b + c), (2 * b + c, 2 * a + c))]
        return lax.ppermute(x, "sweep", pairs)

    def exchange(blocks):
        return lax.all_to_all(blocks, "layer", 0, 0, tiled=True)

    down_own = down_source.reshape(rhs, rows)
    down_got = swap(down_own[:, :wide])
    received = swap(second_halves(matrix, chips))
    base_a = jnp.where(on_0, down_own[:, wide:], down_got)
    base_b = jnp.where(on_0, down_got, down_own[:, wide:])
    up_own = up_source.reshape(rhs, rows)
    up_other = swap(up_own)
    up_a = jnp.where(on_0, up_own[:, :wide], up_other[:, wide:])
    up_b_rest = jnp.where(on_0, up_other[:, :wide], up_own[:, wide:])

    core = (me % 2).astype(jnp.int32).reshape(1)
    tie = lambda *values: lax.optimization_barrier(values)

    flops = 8 * rhs * rows * cols // 2
    part = jax.ShapeDtypeStruct((rhs, wide), F32)
    down_call = vmem_call(down_body, (part, part), "down_product", flops)
    up_call = vmem_call(up_body, jax.ShapeDtypeStruct((chips, rhs, wide), BF16), "up_product", flops)

    def spread(x):
        return exchange(jnp.broadcast_to(x.astype(BF16), (chips, rhs, wide)))

    def down_product(blocks, mat, keeps_first, base):
        mine, theirs = down_call(blocks, mat, keeps_first, base)
        return mine + swap(theirs)

    def up_product(x, other, first_on_0, mat, base):
        x, other = x.astype(BF16), other.astype(BF16)
        halves = [jnp.where(on_0, x, other), jnp.where(on_0, other, x)]
        full = jnp.concatenate(halves if first_on_0 else halves[::-1], axis=1)
        blocks = exchange(up_call(full, mat))
        return base + jnp.sum(blocks.astype(F32), axis=0)

    down_a, down_b = base_a, base_b
    matrix_a = matrix_b = None
    x, tile_0, tile_1, on_0, masks = tie(base_a, tile_0, tile_1, on_0, masks)
    for p in range(planes):
        if p > 0:
            if p == 1:
                matrix_a = load_half(core, 0, matrix, received, x, chips)
            x = hop(x.astype(BF16), p - 1, p)
            if p == 1:
                x, matrix_a, up_a, up_b_rest = tie(x, matrix_a, up_a, up_b_rest)
            x = down_product(spread(x), matrix_a, tile_1, base_a)
            down_a = jnp.where(masks[p], x, down_a)
        blocks = spread(x)
        if p == 0:
            matrix_b = load_half(core, 1, matrix, received, blocks, chips)
        x = down_product(blocks, matrix_b, tile_0, base_b)
        down_b = jnp.where(masks[p], x, down_b)

    rest = up_b_rest + down_b
    base_b = swap(rest)
    base_a = up_a + swap(down_a)
    base_a, base_b, rest = tie(base_a, base_b, rest)
    total_a, total_b = base_a, base_b
    x = None
    for p in reversed(range(planes)):
        if p < planes - 1:
            x = hop(x.astype(BF16), p + 1, p)
            x = up_product(x, swap(x), True, matrix_b, base_b)
            total_b = jnp.where(masks[p], x, total_b)
            other = swap(x.astype(BF16))
        else:
            x, other = base_b, rest
        x = up_product(x, other, False, matrix_a, base_a)
        total_a = jnp.where(masks[p], x, total_a)

    got = swap(jnp.where(on_0, total_b, total_a))
    out = jnp.concatenate([jnp.where(on_0, total_a, total_b), got], axis=1)
    return out.reshape(1, 2, rhs // 2, rows)


def solution(mesh):
    in_specs = (
        P("sweep", None, "layer", None),
        P("sweep", None, None, "layer"),
        P("sweep", None, None, "layer"),
    )
    out_specs = P("sweep", None, None, "layer")
    return jax.shard_map(local, mesh=mesh, in_specs=in_specs, out_specs=out_specs, check_vma=False)
```

```python
import jax
import jax.numpy as jnp
from jax import lax
from jax.experimental import pallas as pl
from jax.experimental.pallas import tpu as pltpu
from jax.sharding import PartitionSpec as P

F32, BF16 = jnp.float32, jnp.bfloat16
MIB = 1 << 20
VMEM = pl.BlockSpec(memory_space=pltpu.VMEM)
HBM = pl.BlockSpec(memory_space=pltpu.HBM)
SMEM = pl.BlockSpec(memory_space=pltpu.SMEM)


def copy_all(copies):
    for copy in copies:
        copy.start()
    for copy in copies:
        copy.wait()


def second_halves(matrix, chips):
    parts, rows, cols = matrix.shape
    wide = cols // (2 * chips)

    def body(matrix_ref, out_ref, held, in_sems, out_sems):
        taken = [
            pltpu.make_async_copy(
                matrix_ref.at[:, :, pl.ds((2 * i + 1) * wide, wide)], held.at[i], in_sems.at[i]
            )
            for i in range(chips)
        ]
        put = [
            pltpu.make_async_copy(
                held.at[i], out_ref.at[:, :, pl.ds(i * wide, wide)], out_sems.at[i]
            )
            for i in range(chips)
        ]
        for copy in taken:
            copy.start()
        for i in range(chips):
            taken[i].wait()
            put[i].start()
        for copy in put:
            copy.wait()

    return pl.pallas_call(
        body,
        in_specs=[HBM],
        out_specs=HBM,
        out_shape=pltpu.HBM((parts, rows, cols // 2), BF16),
        scratch_shapes=[
            pltpu.VMEM((chips, parts, rows, wide), BF16),
            pltpu.SemaphoreType.DMA((chips,)),
            pltpu.SemaphoreType.DMA((chips,)),
        ],
        compiler_params=pltpu.CompilerParams(vmem_limit_bytes=56 * MIB),
        name="second_halves",
    )(matrix)


def load_half(core, on_core, matrix, received, after, chips):
    parts, rows, cols = matrix.shape
    wide = cols // (2 * chips)

    def body(core_ref, matrix_ref, received_ref, after_ref, out_ref, sems):
        @pl.when(core_ref[0] == on_core)
        def _():
            copy_all(
                [
                    pltpu.make_async_copy(
                        matrix_ref.at[:, :, pl.ds(2 * i * wide, wide)],
                        out_ref.at[:, :, pl.ds(i * wide, wide)],
                        sems.at[i],
                    )
                    for i in range(chips)
                ]
            )

        @pl.when(core_ref[0] != on_core)
        def _():
            copy_all(
                [
                    pltpu.make_async_copy(
                        received_ref.at[:, :, pl.ds(i * wide, wide)],
                        out_ref.at[:, :, pl.ds(i * wide, wide)],
                        sems.at[i],
                    )
                    for i in range(chips)
                ]
            )

    return pl.pallas_call(
        body,
        in_specs=[SMEM, HBM, HBM, VMEM],
        out_specs=VMEM,
        out_shape=pltpu.VMEM((parts, rows, cols // 2), BF16),
        scratch_shapes=[pltpu.SemaphoreType.DMA((chips,))],
        compiler_params=pltpu.CompilerParams(vmem_limit_bytes=40 * MIB),
        name="load_half",
    )(core, matrix, received, after)


def vmem_call(body, out_shape, name, flops):
    def call(*args):
        return pl.pallas_call(
            body,
            in_specs=[VMEM] * len(args),
            out_specs=jax.tree.map(lambda _: VMEM, out_shape),
            out_shape=out_shape,
            compiler_params=pltpu.CompilerParams(vmem_limit_bytes=8 * MIB),
            cost_estimate=pl.CostEstimate(flops=flops, bytes_accessed=1 << 16, transcendentals=0),
            name=name,
        )(*args)

    return call


def down_body(x_ref, g_ref, first_ref, base_ref, mine_ref, theirs_ref):
    chips, rhs, wide = x_ref.shape
    contract = (((1,), (1,)), ((), ()))
    with_real = with_imag = None
    for i in range(chips):
        at = slice(i * wide, (i + 1) * wide)
        r = lax.dot_general(x_ref[i], g_ref[0, :, at], contract, preferred_element_type=F32)
        m = lax.dot_general(x_ref[i], g_ref[1, :, at], contract, preferred_element_type=F32)
        with_real = r if i == 0 else with_real + r
        with_imag = m if i == 0 else with_imag + m
    n = rhs // 2
    real = with_real[:n] - with_imag[n:]
    imag = with_imag[:n] + with_real[n:]
    first = jnp.concatenate([real[:, :wide], imag[:, :wide]], axis=0)
    second = jnp.concatenate([real[:, wide:], imag[:, wide:]], axis=0)
    keeps_first = first_ref[0:1, 0:1] == 1
    mine_ref[...] = jnp.where(keeps_first, first, second) + base_ref[...]
    theirs_ref[...] = jnp.where(keeps_first, second, first)


def up_body(x_ref, g_ref, out_ref):
    chips, rhs, wide = out_ref.shape
    n = rhs // 2
    x = x_ref[...]
    for i in range(chips):
        at = slice(i * wide, (i + 1) * wide)
        r = jnp.dot(x, g_ref[0, :, at], preferred_element_type=F32)
        m = jnp.dot(x, g_ref[1, :, at], preferred_element_type=F32)
        out_ref[i, :n] = (r[:n] - m[n:]).astype(BF16)
        out_ref[i, n:] = (m[:n] + r[n:]).astype(BF16)


def make_masks(me, count, shape):
    def body(me_ref, out_ref):
        index = me_ref[0]
        for p in range(count):
            out_ref[p] = jnp.full(shape, jnp.where(index // 2 == p, 1, 0), jnp.int32)
        out_ref[count] = jnp.full(shape, jnp.where(index % 2 == 0, 1, 0), jnp.int32)

    return pl.pallas_call(
        body,
        in_specs=[SMEM],
        out_specs=VMEM,
        out_shape=pltpu.VMEM((count + 1, *shape), jnp.int32),
        name="make_masks",
    )(me)


def local(green, down_source, up_source):
    planes = lax.axis_size("sweep") // 2
    chips = lax.axis_size("layer")
    matrix = green[0]
    rows, cols = matrix.shape[1:]
    wide = rows // 2
    rhs = 2 * down_source.shape[2]
    me = lax.axis_index("sweep")
    masks = make_masks(me.astype(jnp.int32).reshape(1), planes, (rhs, wide))
    tile_0 = masks[planes, :8, :128]
    tile_1 = 1 - tile_0
    masks = [masks[p] == 1 for p in range(planes + 1)]
    on_0 = masks.pop()

    def swap(x):
        return lax.ppermute(x, "sweep", [(i, i ^ 1) for i in range(2 * planes)])

    def hop(x, a, b):
        pairs = [p for c in range(2) for p in ((2 * a + c, 2 * b + c), (2 * b + c, 2 * a + c))]
        return lax.ppermute(x, "sweep", pairs)

    def exchange(blocks):
        return lax.all_to_all(blocks, "layer", 0, 0, tiled=True)

    down_own = down_source.reshape(rhs, rows)
    down_got = swap(down_own[:, :wide])
    tie = lambda *values: lax.optimization_barrier(values)
    sent, down_got = tie(second_halves(matrix, chips), down_got)
    received = swap(sent)
    base_a = jnp.where(on_0, down_own[:, wide:], down_got)
    base_b = jnp.where(on_0, down_got, down_own[:, wide:])
    up_own = up_source.reshape(rhs, rows)

    core = (me % 2).astype(jnp.int32).reshape(1)

    flops = 8 * rhs * rows * cols // 2
    part = jax.ShapeDtypeStruct((rhs, wide), F32)
    down_call = vmem_call(down_body, (part, part), "down_product", flops)
    up_call = vmem_call(up_body, jax.ShapeDtypeStruct((chips, rhs, wide), BF16), "up_product", flops)

    def spread(x):
        return exchange(jnp.broadcast_to(x.astype(BF16), (chips, rhs, wide)))

    def down_product(blocks, mat, keeps_first, base):
        mine, theirs = down_call(blocks, mat, keeps_first, base)
        return mine + swap(theirs)

    def up_product(x, other, first_on_0, mat, base):
        x, other = x.astype(BF16), other.astype(BF16)
        halves = [jnp.where(on_0, x, other), jnp.where(on_0, other, x)]
        full = jnp.concatenate(halves if first_on_0 else halves[::-1], axis=1)
        blocks = exchange(up_call(full, mat))
        return base + jnp.sum(blocks.astype(F32), axis=0)

    down_a, down_b = base_a, base_b
    matrix_a = matrix_b = None
    x, tile_0, tile_1, on_0, masks = tie(base_a, tile_0, tile_1, on_0, masks)
    for p in range(planes):
        if p > 0:
            if p == 1:
                matrix_a = load_half(core, 0, matrix, received, x, chips)
                x, up_own = tie(x, up_own)
                up_other = swap(up_own)
                up_a = jnp.where(on_0, up_own[:, :wide], up_other[:, wide:])
                up_b_rest = jnp.where(on_0, up_other[:, :wide], up_own[:, wide:])
            x = hop(x.astype(BF16), p - 1, p)
            if p == 1:
                x, matrix_a, up_a, up_b_rest = tie(x, matrix_a, up_a, up_b_rest)
            x = down_product(spread(x), matrix_a, tile_1, base_a)
            down_a = jnp.where(masks[p], x, down_a)
        blocks = spread(x)
        if p == 0:
            matrix_b = load_half(core, 1, matrix, received, blocks, chips)
        x = down_product(blocks, matrix_b, tile_0, base_b)
        down_b = jnp.where(masks[p], x, down_b)

    rest = up_b_rest + down_b
    base_b = swap(rest)
    base_a = up_a + swap(down_a)
    base_a, base_b, rest = tie(base_a, base_b, rest)
    total_a, total_b = base_a, base_b
    x = None
    for p in reversed(range(planes)):
        if p < planes - 1:
            x = hop(x.astype(BF16), p + 1, p)
            x = up_product(x, swap(x), True, matrix_b, base_b)
            total_b = jnp.where(masks[p], x, total_b)
            other = swap(x.astype(BF16))
        else:
            x, other = base_b, rest
        x = up_product(x, other, False, matrix_a, base_a)
        total_a = jnp.where(masks[p], x, total_a)

    got = swap(jnp.where(on_0, total_b, total_a))
    out = jnp.concatenate([jnp.where(on_0, total_a, total_b), got], axis=1)
    return out.reshape(1, 2, rhs // 2, rows)


def solution(mesh):
    in_specs = (
        P("sweep", None, "layer", None),
        P("sweep", None, None, "layer"),
        P("sweep", None, None, "layer"),
    )
    out_specs = P("sweep", None, None, "layer")
    return jax.shard_map(local, mesh=mesh, in_specs=in_specs, out_specs=out_specs, check_vma=False)
```

```python
import jax
import jax.numpy as jnp
from jax import lax
from jax.experimental import pallas as pl
from jax.experimental.pallas import tpu as pltpu
from jax.sharding import PartitionSpec as P

F32, BF16 = jnp.float32, jnp.bfloat16
MIB = 1 << 20
VMEM = pl.BlockSpec(memory_space=pltpu.VMEM)
HBM = pl.BlockSpec(memory_space=pltpu.HBM)
SMEM = pl.BlockSpec(memory_space=pltpu.SMEM)


def down_sums(x, g, sums):
    contract = (((1,), (1,)), ((), ()))
    r = lax.dot_general(x, g[0], contract, preferred_element_type=F32)
    m = lax.dot_general(x, g[1], contract, preferred_element_type=F32)
    return (r, m) if sums is None else (sums[0] + r, sums[1] + m)


def complex_of(sums, n):
    with_real, with_imag = sums
    return with_real[:n] - with_imag[n:], with_imag[:n] + with_real[n:]


def write_down(sums, first_ref, base_ref, mine_ref, theirs_ref):
    n, wide = base_ref.shape[0] // 2, base_ref.shape[1]
    real, imag = complex_of(sums, n)
    first = jnp.concatenate([real[:, :wide], imag[:, :wide]], axis=0)
    second = jnp.concatenate([real[:, wide:], imag[:, wide:]], axis=0)
    keeps_first = first_ref[0:1, 0:1] == 1
    mine_ref[...] = jnp.where(keeps_first, first, second) + base_ref[...]
    theirs_ref[...] = jnp.where(keeps_first, second, first)


def whole_product(blocks, matrix):
    chips, rhs, wide = blocks.shape
    parts, rows, cols = matrix.shape

    def body(x_ref, matrix_ref, out_ref, held, sems):
        copies = [
            pltpu.make_async_copy(matrix_ref.at[:, :, pl.ds(i * wide, wide)], held.at[i], sems.at[i])
            for i in range(chips)
        ]
        for copy in copies:
            copy.start()
        sums = None
        for i in range(chips):
            copies[i].wait()
            sums = down_sums(x_ref[i], held.at[i], sums)
        out_ref[...] = jnp.concatenate(complex_of(sums, rhs // 2), axis=0)

    return pl.pallas_call(
        body,
        in_specs=[VMEM, HBM],
        out_specs=VMEM,
        out_shape=jax.ShapeDtypeStruct((rhs, rows), F32),
        scratch_shapes=[
            pltpu.VMEM((chips, parts, rows, wide), BF16),
            pltpu.SemaphoreType.DMA((chips,)),
        ],
        compiler_params=pltpu.CompilerParams(vmem_limit_bytes=56 * MIB),
        cost_estimate=pl.CostEstimate(
            flops=8 * rhs * rows * cols, bytes_accessed=2 * parts * rows * cols, transcendentals=0
        ),
        name="whole_product",
    )(blocks, matrix)


def load_product(me, on_core, matrix, received, blocks, keeps_first, base):
    chips, rhs, wide = blocks.shape
    parts, rows, cols = matrix.shape

    def body(me_ref, matrix_ref, received_ref, x_ref, first_ref, base_ref, mine_ref, theirs_ref, out_ref, sems):
        def copy(source_ref, at, i):
            here = pl.ds(i * wide, wide)
            return pltpu.make_async_copy(source_ref.at[:, :, pl.ds(at, wide)], out_ref.at[:, :, here], sems.at[i])

        @pl.when(me_ref[0] % 2 == on_core)
        def _():
            for i in range(chips):
                copy(matrix_ref, 2 * i * wide, i).start()

        @pl.when(me_ref[0] % 2 != on_core)
        def _():
            for i in range(chips):
                copy(received_ref, (2 * i + 1) * wide, i).start()

        sums = None
        for i in range(chips):
            copy(received_ref, i * wide, i).wait()
            sums = down_sums(x_ref[i], out_ref.at[:, :, pl.ds(i * wide, wide)], sums)
        write_down(sums, first_ref, base_ref, mine_ref, theirs_ref)

    part = jax.ShapeDtypeStruct((rhs, wide), F32)
    return pl.pallas_call(
        body,
        in_specs=[SMEM, HBM, HBM, VMEM, VMEM, VMEM],
        out_specs=[VMEM, VMEM, VMEM],
        out_shape=[part, part, pltpu.VMEM((parts, rows, cols // 2), BF16)],
        scratch_shapes=[pltpu.SemaphoreType.DMA((chips,))],
        compiler_params=pltpu.CompilerParams(vmem_limit_bytes=40 * MIB),
        cost_estimate=pl.CostEstimate(
            flops=4 * rhs * rows * cols, bytes_accessed=parts * rows * cols, transcendentals=0
        ),
        name="load_product",
    )(me, matrix, received, blocks, keeps_first, base)


def vmem_call(body, out_shape, name, flops):
    def call(*args):
        return pl.pallas_call(
            body,
            in_specs=[VMEM] * len(args),
            out_specs=jax.tree.map(lambda _: VMEM, out_shape),
            out_shape=out_shape,
            compiler_params=pltpu.CompilerParams(vmem_limit_bytes=8 * MIB),
            cost_estimate=pl.CostEstimate(flops=flops, bytes_accessed=1 << 16, transcendentals=0),
            name=name,
        )(*args)

    return call


def down_body(x_ref, g_ref, first_ref, base_ref, mine_ref, theirs_ref):
    chips, rhs, wide = x_ref.shape
    sums = None
    for i in range(chips):
        sums = down_sums(x_ref[i], g_ref.at[:, :, pl.ds(i * wide, wide)], sums)
    write_down(sums, first_ref, base_ref, mine_ref, theirs_ref)


def up_body(x_ref, g_ref, out_ref):
    chips, rhs, wide = out_ref.shape
    n = rhs // 2
    x = x_ref[...]
    for i in range(chips):
        at = slice(i * wide, (i + 1) * wide)
        r = jnp.dot(x, g_ref[0, :, at], preferred_element_type=F32)
        m = jnp.dot(x, g_ref[1, :, at], preferred_element_type=F32)
        out_ref[i, :n] = (r[:n] - m[n:]).astype(BF16)
        out_ref[i, n:] = (m[:n] + r[n:]).astype(BF16)


def make_masks(me, count, shape):
    def body(me_ref, out_ref):
        index = me_ref[0]
        for p in range(count):
            out_ref[p] = jnp.full(shape, jnp.where(index // 2 == p, 1, 0), jnp.int32)
        out_ref[count] = jnp.full(shape, jnp.where(index % 2 == 0, 1, 0), jnp.int32)

    return pl.pallas_call(
        body,
        in_specs=[SMEM],
        out_specs=VMEM,
        out_shape=pltpu.VMEM((count + 1, *shape), jnp.int32),
        name="make_masks",
    )(me)


def local(green, down_source, up_source):
    planes = lax.axis_size("sweep") // 2
    chips = lax.axis_size("layer")
    matrix = green[0]
    rows, cols = matrix.shape[1:]
    wide = rows // 2
    rhs = 2 * down_source.shape[2]

    def swap(x):
        return lax.ppermute(x, "sweep", [(i, i ^ 1) for i in range(2 * planes)])

    def trade(x, pairs):
        return lax.ppermute(x, "sweep", [p for a, b in pairs for p in ((a, b), (b, a))])

    def hop(x, a, b):
        return trade(x, [(2 * a + c, 2 * b + c) for c in range(2)])

    def hop_across(x, a, b):
        return trade(x, [(2 * a + c, 2 * b + 1 - c) for c in range(2)])

    def exchange(blocks):
        return lax.all_to_all(blocks, "layer", 0, 0, tiled=True)

    def spread(x):
        return exchange(jnp.broadcast_to(x.astype(BF16), (chips, *x.shape)))

    tie = lambda *values: lax.optimization_barrier(values)
    me = lax.axis_index("sweep").astype(jnp.int32).reshape(1)
    masks = make_masks(me, planes, (rhs, wide))
    tile_0 = masks[planes, :8, :128]
    tile_1 = 1 - tile_0
    masks = [masks[p] == 1 for p in range(planes + 1)]
    on_0 = masks.pop()

    flops = 4 * rhs * rows * cols
    part = jax.ShapeDtypeStruct((rhs, wide), F32)
    down_call = vmem_call(down_body, (part, part), "down_product", flops)
    up_call = vmem_call(up_body, jax.ShapeDtypeStruct((chips, rhs, wide), BF16), "up_product", flops)

    def up_product(x, other, first_on_0, mat, base):
        x, other = x.astype(BF16), other.astype(BF16)
        halves = [jnp.where(on_0, x, other), jnp.where(on_0, other, x)]
        full = jnp.concatenate(halves if first_on_0 else halves[::-1], axis=1)
        blocks = exchange(up_call(full, mat))
        return base + jnp.sum(blocks.astype(F32), axis=0)

    down_own, up_own = down_source.reshape(rhs, rows), up_source.reshape(rhs, rows)
    x = swap(down_own.astype(BF16))
    down_got, up_other = swap(down_own[:, :wide]), swap(up_own)
    x, down_got, up_other, matrix, me, tile_0, tile_1, on_0, masks = tie(
        x, down_got, up_other, matrix, me, tile_0, tile_1, on_0, masks
    )
    received = swap(matrix)
    whole = whole_product(spread(x), matrix) + down_own
    x_1 = trade(whole[:, wide:].astype(BF16), [(1, 3)])
    x_0 = trade(whole[:, :wide].astype(BF16), [(1, 2)])
    base_a = jnp.where(on_0, down_own[:, wide:], down_got)
    base_b = jnp.where(on_0, down_got, down_own[:, wide:])
    up_a = jnp.where(on_0, up_own[:, :wide], up_other[:, wide:])
    up_b = jnp.where(on_0, up_other[:, wide:], up_own[:, :wide])
    up_b_rest = jnp.where(on_0, up_other[:, :wide], up_own[:, wide:])
    down_a = base_a
    x = jnp.where(on_0, x_0, x_1)

    x, base_a, base_b, up_a, up_b, up_b_rest = tie(x, base_a, base_b, up_a, up_b, up_b_rest)
    for p in range(1, planes):
        if p > 1:
            x = hop(x.astype(BF16), p - 1, p)
        if p == 2:
            x, down_b = tie(x, down_b)
        blocks = spread(x)
        if p == 1:
            blocks, received = tie(blocks, received)
            mine, theirs, matrix_a = load_product(me, 0, matrix, received, blocks, tile_1, base_a)
        else:
            mine, theirs = down_call(blocks, matrix_a, tile_1, base_a)
        x = mine + swap(theirs)
        down_a = jnp.where(masks[p], x, down_a)
        blocks = spread(x)
        if p == 1:
            mine, theirs, matrix_b = load_product(me, 1, matrix, received, blocks, tile_0, base_b)
        else:
            mine, theirs = down_call(blocks, matrix_b, tile_0, base_b)
        if p == planes - 1:
            break
        x = mine + swap(theirs)
        if p == 1:
            whole, x = tie(whole, x)
            down_b = jnp.where(on_0, swap(whole[:, :wide]), whole[:, wide:])
        down_b = jnp.where(masks[p], x, down_b)

    mine, theirs, down_a, down_b = tie(mine, theirs, down_a, down_b)
    rest = up_b_rest + (mine + swap(theirs))
    x = up_b + (theirs + swap(mine))
    base_b = up_b + swap(down_b)
    base_a = up_a + swap(down_a)
    x, rest, base_a, base_b = tie(x, rest, base_a, base_b)
    total_a, total_b = base_a, jnp.where(masks[planes - 1], x, base_b)
    for p in reversed(range(planes)):
        if p < planes - 1:
            x = x.astype(BF16)
            x = up_product(hop(x, p + 1, p), hop_across(x, p + 1, p), True, matrix_b, base_b)
            total_b = jnp.where(masks[p], x, total_b)
            rest = swap(x.astype(BF16))
        x = up_product(x, rest, False, matrix_a, base_a)
        total_a = jnp.where(masks[p], x, total_a)

    got = swap(jnp.where(on_0, total_b, total_a))
    out = jnp.concatenate([jnp.where(on_0, total_a, total_b), got], axis=1)
    return out.reshape(1, 2, rhs // 2, rows)


def solution(mesh):
    in_specs = (
        P("sweep", None, "layer", None),
        P("sweep", None, None, "layer"),
        P("sweep", None, None, "layer"),
    )
    out_specs = P("sweep", None, None, "layer")
    return jax.shard_map(local, mesh=mesh, in_specs=in_specs, out_specs=out_specs, check_vma=False)
```

```python
import jax
import jax.numpy as jnp
from jax import lax
from jax.experimental import pallas as pl
from jax.experimental.pallas import tpu as pltpu
from jax.sharding import PartitionSpec as P

F32, BF16 = jnp.float32, jnp.bfloat16
MIB = 1 << 20
VMEM = pl.BlockSpec(memory_space=pltpu.VMEM)
HBM = pl.BlockSpec(memory_space=pltpu.HBM)
SMEM = pl.BlockSpec(memory_space=pltpu.SMEM)


def down_sums(x, g, sums):
    contract = (((1,), (1,)), ((), ()))
    r = lax.dot_general(x, g[0], contract, preferred_element_type=F32)
    m = lax.dot_general(x, g[1], contract, preferred_element_type=F32)
    return (r, m) if sums is None else (sums[0] + r, sums[1] + m)


def complex_of(sums, n):
    with_real, with_imag = sums
    return with_real[:n] - with_imag[n:], with_imag[:n] + with_real[n:]


def write_down(sums, first_ref, base_ref, mine_ref, theirs_ref):
    n, wide = base_ref.shape[0] // 2, base_ref.shape[1]
    real, imag = complex_of(sums, n)
    first = jnp.concatenate([real[:, :wide], imag[:, :wide]], axis=0)
    second = jnp.concatenate([real[:, wide:], imag[:, wide:]], axis=0)
    keeps_first = first_ref[0:1, 0:1] == 1
    mine_ref[...] = jnp.where(keeps_first, first, second) + base_ref[...]
    theirs_ref[...] = jnp.where(keeps_first, second, first)


def second_halves(matrix, first, count, chips):
    parts, rows, cols = matrix.shape
    wide = cols // (2 * chips)

    def body(matrix_ref, out_ref, held, in_sems, out_sems):
        taken, put = [], []
        for i in range(count):
            at = (2 * (first + i) + 1) * wide
            taken.append(
                pltpu.make_async_copy(matrix_ref.at[:, :, pl.ds(at, wide)], held.at[i], in_sems.at[i])
            )
            put.append(
                pltpu.make_async_copy(held.at[i], out_ref.at[:, :, pl.ds(i * wide, wide)], out_sems.at[i])
            )
        for copy in taken:
            copy.start()
        for i in range(count):
            taken[i].wait()
            put[i].start()
        for copy in put:
            copy.wait()

    return pl.pallas_call(
        body,
        in_specs=[HBM],
        out_specs=HBM,
        out_shape=pltpu.HBM((parts, rows, count * wide), BF16),
        scratch_shapes=[
            pltpu.VMEM((count, parts, rows, wide), BF16),
            pltpu.SemaphoreType.DMA((count,)),
            pltpu.SemaphoreType.DMA((count,)),
        ],
        compiler_params=pltpu.CompilerParams(vmem_limit_bytes=56 * MIB),
        name="second_halves",
    )(matrix)


def load_product(me, on_core, matrix, received, blocks, keeps_first, base):
    chips, rhs, wide = blocks.shape
    parts, rows, cols = matrix.shape

    pieces = len(received)
    per = chips // pieces

    def body(me_ref, matrix_ref, *refs):
        received_refs = refs[:pieces]
        x_ref, first_ref, base_ref, mine_ref, theirs_ref, out_ref, sems = refs[pieces:]

        def copy(source_ref, at, i):
            here = pl.ds(i * wide, wide)
            return pltpu.make_async_copy(source_ref.at[:, :, pl.ds(at, wide)], out_ref.at[:, :, here], sems.at[i])

        @pl.when(me_ref[0] % 2 == on_core)
        def _():
            for i in range(chips):
                copy(matrix_ref, 2 * i * wide, i).start()

        @pl.when(me_ref[0] % 2 != on_core)
        def _():
            for i in range(chips):
                copy(received_refs[i // per], i % per * wide, i).start()

        sums = None
        for i in range(chips):
            copy(matrix_ref, i * wide, i).wait()
            sums = down_sums(x_ref[i], out_ref.at[:, :, pl.ds(i * wide, wide)], sums)
        write_down(sums, first_ref, base_ref, mine_ref, theirs_ref)

    part = jax.ShapeDtypeStruct((rhs, wide), F32)
    return pl.pallas_call(
        body,
        in_specs=[SMEM, HBM, *[HBM] * pieces, VMEM, VMEM, VMEM],
        out_specs=[VMEM, VMEM, VMEM],
        out_shape=[part, part, pltpu.VMEM((parts, rows, cols // 2), BF16)],
        scratch_shapes=[pltpu.SemaphoreType.DMA((chips,))],
        compiler_params=pltpu.CompilerParams(vmem_limit_bytes=40 * MIB),
        cost_estimate=pl.CostEstimate(
            flops=4 * rhs * rows * cols, bytes_accessed=parts * rows * cols, transcendentals=0
        ),
        name="load_product",
    )(me, matrix, *received, blocks, keeps_first, base)


def vmem_call(body, out_shape, name, flops):
    def call(*args):
        return pl.pallas_call(
            body,
            in_specs=[VMEM] * len(args),
            out_specs=jax.tree.map(lambda _: VMEM, out_shape),
            out_shape=out_shape,
            compiler_params=pltpu.CompilerParams(vmem_limit_bytes=8 * MIB),
            cost_estimate=pl.CostEstimate(flops=flops, bytes_accessed=1 << 16, transcendentals=0),
            name=name,
        )(*args)

    return call


def down_body(x_ref, g_ref, first_ref, base_ref, mine_ref, theirs_ref):
    chips, rhs, wide = x_ref.shape
    sums = None
    for i in range(chips):
        sums = down_sums(x_ref[i], g_ref.at[:, :, pl.ds(i * wide, wide)], sums)
    write_down(sums, first_ref, base_ref, mine_ref, theirs_ref)


def up_body(x_ref, g_ref, out_ref):
    chips, rhs, wide = out_ref.shape
    n = rhs // 2
    x = x_ref[...]
    for i in range(chips):
        at = slice(i * wide, (i + 1) * wide)
        r = jnp.dot(x, g_ref[0, :, at], preferred_element_type=F32)
        m = jnp.dot(x, g_ref[1, :, at], preferred_element_type=F32)
        out_ref[i, :n] = (r[:n] - m[n:]).astype(BF16)
        out_ref[i, n:] = (m[:n] + r[n:]).astype(BF16)


def make_masks(me, count, shape):
    def body(me_ref, out_ref):
        index = me_ref[0]
        for p in range(count):
            out_ref[p] = jnp.full(shape, jnp.where(index // 2 == p, 1, 0), jnp.int32)
        out_ref[count] = jnp.full(shape, jnp.where(index % 2 == 0, 1, 0), jnp.int32)

    return pl.pallas_call(
        body,
        in_specs=[SMEM],
        out_specs=VMEM,
        out_shape=pltpu.VMEM((count + 1, *shape), jnp.int32),
        name="make_masks",
    )(me)


def local(green, down_source, up_source):
    planes = lax.axis_size("sweep") // 2
    chips = lax.axis_size("layer")
    matrix = green[0]
    rows, cols = matrix.shape[1:]
    wide = rows // 2
    rhs = 2 * down_source.shape[2]

    def swap(x):
        return lax.ppermute(x, "sweep", [(i, i ^ 1) for i in range(2 * planes)])

    def hop(x, a, b):
        pairs = [p for c in range(2) for p in ((2 * a + c, 2 * b + c), (2 * b + c, 2 * a + c))]
        return lax.ppermute(x, "sweep", pairs)

    def exchange(blocks):
        return lax.all_to_all(blocks, "layer", 0, 0, tiled=True)

    def spread(x):
        return exchange(jnp.broadcast_to(x.astype(BF16), (chips, *x.shape)))

    tie = lambda *values: lax.optimization_barrier(values)
    me = lax.axis_index("sweep").astype(jnp.int32).reshape(1)
    masks = make_masks(me, planes, (rhs, wide))
    tile_0 = masks[planes, :8, :128]
    tile_1 = 1 - tile_0
    masks = [masks[p] == 1 for p in range(planes + 1)]
    on_0 = masks.pop()

    flops = 4 * rhs * rows * cols
    part = jax.ShapeDtypeStruct((rhs, wide), F32)
    down_call = vmem_call(down_body, (part, part), "down_product", flops)
    up_call = vmem_call(up_body, jax.ShapeDtypeStruct((chips, rhs, wide), BF16), "up_product", flops)

    def ordered(x, other, first_on_0):
        halves = [jnp.where(on_0, x, other), jnp.where(on_0, other, x)]
        return jnp.concatenate(halves if first_on_0 else halves[::-1], axis=1).astype(BF16)

    def up_product(full, mat, base):
        return base + jnp.sum(exchange(up_call(full, mat)).astype(F32), axis=0)

    down_own, up_own = down_source.reshape(rhs, rows), up_source.reshape(rhs, rows)
    down_got, matrix = tie(swap(down_own[:, :wide]), matrix)
    pieces = 1
    received = [
        swap(second_halves(matrix, j * chips // pieces, chips // pieces, chips)) for j in range(pieces)
    ]
    base_a = jnp.where(on_0, down_own[:, wide:], down_got)
    base_b = jnp.where(on_0, down_got, down_own[:, wide:])
    down_a, down_b = base_a, base_b

    x, me, tile_0, tile_1, on_0, masks = tie(base_a, me, tile_0, tile_1, on_0, masks)
    for p in range(planes):
        if p > 0:
            x = hop(x.astype(BF16), p - 1, p)
            if p == 1:
                x, up_a, up_b, up_b_rest = tie(x, up_a, up_b, up_b_rest)
                mine, theirs, matrix_a = load_product(me, 0, matrix, received, spread(x), tile_1, base_a)
            else:
                mine, theirs = down_call(spread(x), matrix_a, tile_1, base_a)
            x = mine + swap(theirs)
            down_a = jnp.where(masks[p], x, down_a)
        blocks = spread(x)
        if p == 0:
            mine, theirs, matrix_b = load_product(me, 1, matrix, received, blocks, tile_0, base_b)
        else:
            mine, theirs = down_call(blocks, matrix_b, tile_0, base_b)
        if p == planes - 1:
            break
        x = mine + swap(theirs)
        down_b = jnp.where(masks[p], x, down_b)
        if p == 0:
            x, up_own = tie(x, up_own)
            up_other = swap(up_own)
            up_a = jnp.where(on_0, up_own[:, :wide], up_other[:, wide:])
            up_b = jnp.where(on_0, up_other[:, wide:], up_own[:, :wide])
            up_b_rest = jnp.where(on_0, up_other[:, :wide], up_own[:, wide:])

    mine, theirs, down_a, down_b = tie(mine, theirs, down_a, down_b)
    rest = up_b_rest + (mine + swap(theirs))
    x = up_b + (theirs + swap(mine))
    base_b = up_b + swap(down_b)
    base_a = up_a + swap(down_a)
    x, rest, base_a, base_b = tie(x, rest, base_a, base_b)
    total_a, total_b = base_a, jnp.where(masks[planes - 1], x, base_b)
    full = ordered(x, rest, False)
    for p in reversed(range(planes)):
        if p < planes - 1:
            x = up_product(hop(full, p + 1, p), matrix_b, base_b)
            total_b = jnp.where(masks[p], x, total_b)
            full = ordered(x.astype(BF16), swap(x.astype(BF16)), False)
        x = up_product(full, matrix_a, base_a)
        total_a = jnp.where(masks[p], x, total_a)
        if p > 0:
            full = ordered(x.astype(BF16), swap(x.astype(BF16)), True)

    got = swap(jnp.where(on_0, total_b, total_a))
    out = jnp.concatenate([jnp.where(on_0, total_a, total_b), got], axis=1)
    return out.reshape(1, 2, rhs // 2, rows)


def solution(mesh):
    in_specs = (
        P("sweep", None, "layer", None),
        P("sweep", None, None, "layer"),
        P("sweep", None, None, "layer"),
    )
    out_specs = P("sweep", None, None, "layer")
    return jax.shard_map(local, mesh=mesh, in_specs=in_specs, out_specs=out_specs, check_vma=False)
```

```python
import jax
import jax.numpy as jnp
from jax import lax
from jax.experimental import pallas as pl
from jax.experimental.pallas import tpu as pltpu
from jax.sharding import PartitionSpec as P

F32, BF16 = jnp.float32, jnp.bfloat16
MIB = 1 << 20
VMEM = pl.BlockSpec(memory_space=pltpu.VMEM)
HBM = pl.BlockSpec(memory_space=pltpu.HBM)
SMEM = pl.BlockSpec(memory_space=pltpu.SMEM)


def down_sums(x, g, sums):
    contract = (((1,), (1,)), ((), ()))
    r = lax.dot_general(x, g[0], contract, preferred_element_type=F32)
    m = lax.dot_general(x, g[1], contract, preferred_element_type=F32)
    return (r, m) if sums is None else (sums[0] + r, sums[1] + m)


def complex_of(sums, n):
    with_real, with_imag = sums
    return with_real[:n] - with_imag[n:], with_imag[:n] + with_real[n:]


def write_down(sums, first_ref, base_ref, mine_ref, theirs_ref):
    n, wide = base_ref.shape[0] // 2, base_ref.shape[1]
    real, imag = complex_of(sums, n)
    first = jnp.concatenate([real[:, :wide], imag[:, :wide]], axis=0)
    second = jnp.concatenate([real[:, wide:], imag[:, wide:]], axis=0)
    keeps_first = first_ref[0:1, 0:1] == 1
    mine_ref[...] = jnp.where(keeps_first, first, second) + base_ref[...]
    theirs_ref[...] = jnp.where(keeps_first, second, first)


def second_halves(matrix, first, count, chips):
    parts, rows, cols = matrix.shape
    wide = cols // (2 * chips)

    def body(matrix_ref, out_ref, held, in_sems, out_sems):
        taken, put = [], []
        for i in range(count):
            at = (2 * (first + i) + 1) * wide
            taken.append(
                pltpu.make_async_copy(matrix_ref.at[:, :, pl.ds(at, wide)], held.at[i], in_sems.at[i])
            )
            put.append(
                pltpu.make_async_copy(held.at[i], out_ref.at[:, :, pl.ds(i * wide, wide)], out_sems.at[i])
            )
        for copy in taken:
            copy.start()
        for i in range(count):
            taken[i].wait()
            put[i].start()
        for copy in put:
            copy.wait()

    return pl.pallas_call(
        body,
        in_specs=[HBM],
        out_specs=HBM,
        out_shape=pltpu.HBM((parts, rows, count * wide), BF16),
        scratch_shapes=[
            pltpu.VMEM((count, parts, rows, wide), BF16),
            pltpu.SemaphoreType.DMA((count,)),
            pltpu.SemaphoreType.DMA((count,)),
        ],
        compiler_params=pltpu.CompilerParams(vmem_limit_bytes=56 * MIB),
        name="second_halves",
    )(matrix)


def load_product(me, on_core, late, matrix, received, blocks, keeps_first, base):
    chips, rhs, wide = blocks.shape
    parts, rows, cols = matrix.shape

    def body(me_ref, matrix_ref, received_ref, x_ref, first_ref, base_ref, mine_ref, theirs_ref, out_ref, sems):
        index = me_ref[0]

        def copy(source_ref, at, i):
            here = pl.ds(i * wide, wide)
            return pltpu.make_async_copy(source_ref.at[:, :, pl.ds(at, wide)], out_ref.at[pl.ds(0, parts), :, here], sems.at[i])

        @pl.when(index % 2 == on_core)
        def _():
            for i in range(chips):
                copy(matrix_ref, 2 * i * wide, i).start()

        @pl.when(index % 2 != on_core)
        def _():
            for i in range(chips):
                copy(received_ref, i * wide, i).start()

        @pl.when(index < late)
        def _():
            sums = None
            for i in range(chips):
                copy(matrix_ref, i * wide, i).wait()
                sums = down_sums(x_ref[i], out_ref.at[:, :, pl.ds(i * wide, wide)], sums)
            write_down(sums, first_ref, base_ref, mine_ref, theirs_ref)

        @pl.when(index >= late)
        def _():
            for i in range(chips):
                copy(matrix_ref, i * wide, i).wait()
                at = slice(i * wide, (i + 1) * wide)
                for part in range(parts):
                    turned = out_ref[part, :, at].T
                    out_ref[parts + part, :wide, at] = turned[:, :wide]
                    out_ref[parts + part, wide:, at] = turned[:, wide:]
            mine_ref[...] = base_ref[...]
            theirs_ref[...] = base_ref[...]

    part = jax.ShapeDtypeStruct((rhs, wide), F32)
    return pl.pallas_call(
        body,
        in_specs=[SMEM, HBM, HBM, VMEM, VMEM, VMEM],
        out_specs=[VMEM] * 3,
        out_shape=[part, part, pltpu.VMEM((2 * parts, rows, cols // 2), BF16)],
        scratch_shapes=[pltpu.SemaphoreType.DMA((chips,))],
        compiler_params=pltpu.CompilerParams(vmem_limit_bytes=(16 if on_core == 0 else 32) * MIB),
        cost_estimate=pl.CostEstimate(
            flops=4 * rhs * rows * cols, bytes_accessed=parts * rows * cols, transcendentals=0
        ),
        name="load_product",
    )(me, matrix, received, blocks, keeps_first, base)


def vmem_call(body, out_shape, name, flops):
    def call(*args):
        return pl.pallas_call(
            body,
            in_specs=[VMEM] * len(args),
            out_specs=jax.tree.map(lambda _: VMEM, out_shape),
            out_shape=out_shape,
            compiler_params=pltpu.CompilerParams(vmem_limit_bytes=8 * MIB),
            cost_estimate=pl.CostEstimate(flops=flops, bytes_accessed=1 << 16, transcendentals=0),
            name=name,
        )(*args)

    return call


def down_body(x_ref, g_ref, first_ref, base_ref, mine_ref, theirs_ref):
    chips, rhs, wide = x_ref.shape
    sums = None
    for i in range(chips):
        sums = down_sums(x_ref[i], g_ref.at[:, :, pl.ds(i * wide, wide)], sums)
    write_down(sums, first_ref, base_ref, mine_ref, theirs_ref)


def turned_body(x_ref, g_ref, first_ref, base_ref, mine_ref, theirs_ref):
    chips, rhs, wide = x_ref.shape
    sums = None
    for i in range(chips):
        at = slice(i * wide, (i + 1) * wide)
        terms = [
            jnp.concatenate(
                [jnp.dot(x_ref[i], g_ref[part, rows, at], preferred_element_type=F32) for rows in (slice(0, wide), slice(wide, 2 * wide))],
                axis=1,
            )
            for part in (2, 3)
        ]
        sums = terms if sums is None else [total + term for total, term in zip(sums, terms)]
    write_down(sums, first_ref, base_ref, mine_ref, theirs_ref)


def up_body(x_ref, g_ref, out_ref):
    chips, rhs, wide = out_ref.shape
    n = rhs // 2
    x = x_ref[...]
    for i in range(chips):
        at = slice(i * wide, (i + 1) * wide)
        r = jnp.dot(x, g_ref[0, :, at], preferred_element_type=F32)
        m = jnp.dot(x, g_ref[1, :, at], preferred_element_type=F32)
        out_ref[i, :n] = (r[:n] - m[n:]).astype(BF16)
        out_ref[i, n:] = (m[:n] + r[n:]).astype(BF16)


def make_masks(me, count, shape):
    def body(me_ref, out_ref):
        index = me_ref[0]
        for p in range(count):
            out_ref[p] = jnp.full(shape, jnp.where(index // 2 == p, 1, 0), jnp.int32)
        out_ref[count] = jnp.full(shape, jnp.where(index % 2 == 0, 1, 0), jnp.int32)

    return pl.pallas_call(
        body,
        in_specs=[SMEM],
        out_specs=VMEM,
        out_shape=pltpu.VMEM((count + 1, *shape), jnp.int32),
        name="make_masks",
    )(me)


def local(green, down_source, up_source):
    planes = lax.axis_size("sweep") // 2
    chips = lax.axis_size("layer")
    matrix = green[0]
    rows, cols = matrix.shape[1:]
    wide = rows // 2
    rhs = 2 * down_source.shape[2]

    def swap(x):
        return lax.ppermute(x, "sweep", [(i, i ^ 1) for i in range(2 * planes)])

    def hop(x, a, b):
        pairs = [p for c in range(2) for p in ((2 * a + c, 2 * b + c), (2 * b + c, 2 * a + c))]
        return lax.ppermute(x, "sweep", pairs)

    def exchange(blocks):
        return lax.all_to_all(blocks, "layer", 0, 0, tiled=True)

    def spread(x):
        return exchange(jnp.broadcast_to(x.astype(BF16), (chips, *x.shape)))

    tie = lambda *values: lax.optimization_barrier(values)
    me = lax.axis_index("sweep").astype(jnp.int32).reshape(1)
    masks = make_masks(me, planes, (rhs, wide))
    tile_0 = masks[planes, :8, :128]
    tile_1 = 1 - tile_0
    masks = [masks[p] == 1 for p in range(planes + 1)]
    on_0 = masks.pop()

    flops = 4 * rhs * rows * cols
    part = jax.ShapeDtypeStruct((rhs, wide), F32)
    down_call = vmem_call(down_body, (part, part), "down_product", flops)
    turned_call = vmem_call(turned_body, (part, part), "turned_product", flops)
    up_call = vmem_call(up_body, jax.ShapeDtypeStruct((chips, rhs, wide), BF16), "up_product", flops)

    def ordered(x, other, first_on_0):
        halves = [jnp.where(on_0, x, other), jnp.where(on_0, other, x)]
        return jnp.concatenate(halves if first_on_0 else halves[::-1], axis=1).astype(BF16)

    def up_product(full, mat, base, *beside):
        blocks = up_call(full, mat)
        if beside:
            blocks, base, *beside = tie(blocks, base, *beside)
        x = base + jnp.sum(exchange(blocks).astype(F32), axis=0)
        return (x, base, *beside) if beside else x

    down_own, up_own = down_source.reshape(rhs, rows), up_source.reshape(rhs, rows)
    down_got, up_other = swap(down_own[:, :wide]), swap(up_own)
    sent, down_got, up_other = tie(second_halves(matrix, 0, chips, chips), down_got, up_other)
    received = swap(sent)
    up_a = jnp.where(on_0, up_own[:, :wide], up_other[:, wide:])
    up_b = jnp.where(on_0, up_other[:, wide:], up_own[:, :wide])
    up_b_rest = jnp.where(on_0, up_other[:, :wide], up_own[:, wide:])
    base_a = jnp.where(on_0, down_own[:, wide:], down_got)
    base_b = jnp.where(on_0, down_got, down_own[:, wide:])
    down_a, down_b = base_a, base_b

    x, base_b, up_a, up_b, up_b_rest, me, tile_0, tile_1, on_0, masks = tie(
        base_a, base_b, up_a, up_b, up_b_rest, me, tile_0, tile_1, on_0, masks
    )
    late = 4
    for p in range(planes):
        if p > 0:
            blocks = spread(hop(x.astype(BF16), p - 1, p))
            if p == 1:
                mine, theirs, matrix_a = load_product(
                    me, 0, late, matrix, received, blocks, tile_1, base_a
                )
            else:
                mine, theirs = turned_call(blocks, matrix_a, tile_1, base_a)
            x = mine + swap(theirs)
            down_a = jnp.where(masks[p], x, down_a)
        blocks = spread(x)
        if p == 0:
            mine, theirs, matrix_b = load_product(me, 1, late, matrix, received, blocks, tile_0, base_b)
        elif p == 1:
            mine, theirs = down_call(blocks, matrix_b, tile_0, base_b)
        else:
            mine, theirs = turned_call(blocks, matrix_b, tile_0, base_b)
        if p == planes - 1:
            break
        x = mine + swap(theirs)
        down_b = jnp.where(masks[p], x, down_b)

    mine, theirs, down_a, down_b = tie(mine, theirs, down_a, down_b)
    rest = up_b_rest + (mine + swap(theirs))
    x = up_b + (theirs + swap(mine))
    x, rest, down_a, down_b = tie(x, rest, down_a, down_b)
    base_b = up_b + swap(down_b)
    base_a = up_a + swap(down_a)
    last_b = x
    full = ordered(x, rest, False)
    for p in reversed(range(planes)):
        if p < planes - 1:
            x = up_product(hop(full, p + 1, p), matrix_b, base_b)
            total_b = jnp.where(masks[p], x, total_b)
            full = ordered(x.astype(BF16), swap(x.astype(BF16)), False)
        if p == planes - 1:
            x, base_a, base_b, last_b = up_product(full, matrix_a, base_a, base_b, last_b)
            total_a, total_b = x, jnp.where(masks[p], last_b, base_b)
        else:
            x = up_product(full, matrix_a, base_a)
            total_a = jnp.where(masks[p], x, total_a)
        if p > 0:
            full = ordered(x.astype(BF16), swap(x.astype(BF16)), True)

    got = swap(jnp.where(on_0, total_b, total_a))
    out = jnp.concatenate([jnp.where(on_0, total_a, total_b), got], axis=1)
    return out.reshape(1, 2, rhs // 2, rows)


def solution(mesh):
    in_specs = (
        P("sweep", None, "layer", None),
        P("sweep", None, None, "layer"),
        P("sweep", None, None, "layer"),
    )
    out_specs = P("sweep", None, None, "layer")
    return jax.shard_map(local, mesh=mesh, in_specs=in_specs, out_specs=out_specs, check_vma=False)
```

```python
import jax
import jax.numpy as jnp
from jax import lax
from jax.experimental import pallas as pl
from jax.experimental.pallas import tpu as pltpu
from jax.sharding import PartitionSpec as P

F32, BF16 = jnp.float32, jnp.bfloat16
MIB = 1 << 20
VMEM = pl.BlockSpec(memory_space=pltpu.VMEM)
HBM = pl.BlockSpec(memory_space=pltpu.HBM)
SMEM = pl.BlockSpec(memory_space=pltpu.SMEM)


def down_sums(x, g, sums):
    contract = (((1,), (1,)), ((), ()))
    r = lax.dot_general(x, g[0], contract, preferred_element_type=F32)
    m = lax.dot_general(x, g[1], contract, preferred_element_type=F32)
    return (r, m) if sums is None else (sums[0] + r, sums[1] + m)


def complex_of(sums, n):
    with_real, with_imag = sums
    return with_real[:n] - with_imag[n:], with_imag[:n] + with_real[n:]


def write_down(sums, first_ref, base_ref, mine_ref, theirs_ref):
    n, wide = base_ref.shape[0] // 2, base_ref.shape[1]
    real, imag = complex_of(sums, n)
    first = jnp.concatenate([real[:, :wide], imag[:, :wide]], axis=0)
    second = jnp.concatenate([real[:, wide:], imag[:, wide:]], axis=0)
    keeps_first = first_ref[0:1, 0:1] == 1
    mine_ref[...] = jnp.where(keeps_first, first, second) + base_ref[...]
    theirs_ref[...] = jnp.where(keeps_first, second, first)


def second_halves(matrix, first, count, chips):
    parts, rows, cols = matrix.shape
    wide = cols // (2 * chips)

    def body(matrix_ref, out_ref, held, in_sems, out_sems):
        taken, put = [], []
        for i in range(count):
            at = (2 * (first + i) + 1) * wide
            taken.append(
                pltpu.make_async_copy(matrix_ref.at[:, :, pl.ds(at, wide)], held.at[i], in_sems.at[i])
            )
            put.append(
                pltpu.make_async_copy(held.at[i], out_ref.at[:, :, pl.ds(i * wide, wide)], out_sems.at[i])
            )
        for copy in taken:
            copy.start()
        for i in range(count):
            taken[i].wait()
            put[i].start()
        for copy in put:
            copy.wait()

    return pl.pallas_call(
        body,
        in_specs=[HBM],
        out_specs=HBM,
        out_shape=pltpu.HBM((parts, rows, count * wide), BF16),
        scratch_shapes=[
            pltpu.VMEM((count, parts, rows, wide), BF16),
            pltpu.SemaphoreType.DMA((count,)),
            pltpu.SemaphoreType.DMA((count,)),
        ],
        compiler_params=pltpu.CompilerParams(vmem_limit_bytes=56 * MIB),
        name="second_halves",
    )(matrix)


def load_product(me, on_core, late, matrix, received, blocks, keeps_first, base):
    chips, rhs, wide = blocks.shape
    parts, rows, cols = matrix.shape

    pieces = len(received)

    def body(me_ref, matrix_ref, *refs):
        received_refs = refs[:pieces]
        x_ref, first_ref, base_ref, mine_ref, theirs_ref, out_ref, sems = refs[pieces:]
        index, per = me_ref[0], chips // pieces

        def copy(source_ref, at, i):
            here = pl.ds(i * wide, wide)
            return pltpu.make_async_copy(source_ref.at[:, :, pl.ds(at, wide)], out_ref.at[pl.ds(0, parts), :, here], sems.at[i])

        @pl.when(index % 2 == on_core)
        def _():
            for i in range(chips):
                copy(matrix_ref, 2 * i * wide, i).start()

        @pl.when(index % 2 != on_core)
        def _():
            for i in range(chips):
                copy(received_refs[i // per], i % per * wide, i).start()

        @pl.when(index < late)
        def _():
            sums = None
            for i in range(chips):
                copy(matrix_ref, i * wide, i).wait()
                sums = down_sums(x_ref[i], out_ref.at[:, :, pl.ds(i * wide, wide)], sums)
            write_down(sums, first_ref, base_ref, mine_ref, theirs_ref)

        @pl.when(index >= late)
        def _():
            for i in range(chips):
                copy(matrix_ref, i * wide, i).wait()
                at = slice(i * wide, (i + 1) * wide)
                for part in range(parts):
                    turned = out_ref[part, :, at].T
                    out_ref[parts + part, :wide, at] = turned[:, :wide]
                    out_ref[parts + part, wide:, at] = turned[:, wide:]
            mine_ref[...] = base_ref[...]
            theirs_ref[...] = base_ref[...]

    part = jax.ShapeDtypeStruct((rhs, wide), F32)
    return pl.pallas_call(
        body,
        in_specs=[SMEM, HBM, *[HBM] * pieces, VMEM, VMEM, VMEM],
        out_specs=[VMEM] * 3,
        out_shape=[part, part, pltpu.VMEM((2 * parts, rows, cols // 2), BF16)],
        scratch_shapes=[pltpu.SemaphoreType.DMA((chips,))],
        compiler_params=pltpu.CompilerParams(vmem_limit_bytes=(16 if on_core == 0 else 32) * MIB),
        cost_estimate=pl.CostEstimate(
            flops=4 * rhs * rows * cols, bytes_accessed=parts * rows * cols, transcendentals=0
        ),
        name="load_product",
    )(me, matrix, *received, blocks, keeps_first, base)


def vmem_call(body, out_shape, name, flops):
    def call(*args):
        return pl.pallas_call(
            body,
            in_specs=[VMEM] * len(args),
            out_specs=jax.tree.map(lambda _: VMEM, out_shape),
            out_shape=out_shape,
            compiler_params=pltpu.CompilerParams(vmem_limit_bytes=8 * MIB),
            cost_estimate=pl.CostEstimate(flops=flops, bytes_accessed=1 << 16, transcendentals=0),
            name=name,
        )(*args)

    return call


def down_body(x_ref, g_ref, first_ref, base_ref, mine_ref, theirs_ref):
    chips, rhs, wide = x_ref.shape
    sums = None
    for i in range(chips):
        sums = down_sums(x_ref[i], g_ref.at[:, :, pl.ds(i * wide, wide)], sums)
    write_down(sums, first_ref, base_ref, mine_ref, theirs_ref)


def turned_body(x_ref, g_ref, first_ref, base_ref, mine_ref, theirs_ref):
    chips, rhs, wide = x_ref.shape
    sums = None
    for i in range(chips):
        at = slice(i * wide, (i + 1) * wide)
        terms = [
            jnp.concatenate(
                [jnp.dot(x_ref[i], g_ref[part, rows, at], preferred_element_type=F32) for rows in (slice(0, wide), slice(wide, 2 * wide))],
                axis=1,
            )
            for part in (2, 3)
        ]
        sums = terms if sums is None else [total + term for total, term in zip(sums, terms)]
    write_down(sums, first_ref, base_ref, mine_ref, theirs_ref)


def up_body(x_ref, g_ref, out_ref):
    chips, rhs, wide = out_ref.shape
    n = rhs // 2
    x = x_ref[...]
    for i in range(chips):
        at = slice(i * wide, (i + 1) * wide)
        r = jnp.dot(x, g_ref[0, :, at], preferred_element_type=F32)
        m = jnp.dot(x, g_ref[1, :, at], preferred_element_type=F32)
        out_ref[i, :n] = (r[:n] - m[n:]).astype(BF16)
        out_ref[i, n:] = (m[:n] + r[n:]).astype(BF16)


def make_masks(me, count, shape):
    def body(me_ref, out_ref):
        index = me_ref[0]
        for p in range(count):
            out_ref[p] = jnp.full(shape, jnp.where(index // 2 == p, 1, 0), jnp.int32)
        out_ref[count] = jnp.full(shape, jnp.where(index % 2 == 0, 1, 0), jnp.int32)

    return pl.pallas_call(
        body,
        in_specs=[SMEM],
        out_specs=VMEM,
        out_shape=pltpu.VMEM((count + 1, *shape), jnp.int32),
        name="make_masks",
    )(me)


def local(green, down_source, up_source):
    planes = lax.axis_size("sweep") // 2
    chips = lax.axis_size("layer")
    matrix = green[0]
    rows, cols = matrix.shape[1:]
    wide = rows // 2
    rhs = 2 * down_source.shape[2]

    def swap(x):
        return lax.ppermute(x, "sweep", [(i, i ^ 1) for i in range(2 * planes)])

    def hop(x, a, b):
        pairs = [(2 * a + c, 2 * b + c) for c in range(2)]
        return lax.ppermute(x, "sweep", pairs)

    def exchange(blocks):
        return lax.all_to_all(blocks, "layer", 0, 0, tiled=True)

    def spread(x):
        return exchange(jnp.broadcast_to(x.astype(BF16), (chips, *x.shape)))

    tie = lambda *values: lax.optimization_barrier(values)
    me = lax.axis_index("sweep").astype(jnp.int32).reshape(1)
    masks = make_masks(me, planes, (rhs, wide))
    tile_0 = masks[planes, :8, :128]
    tile_1 = 1 - tile_0
    masks = [masks[p] == 1 for p in range(planes + 1)]
    on_0 = masks.pop()

    flops = 4 * rhs * rows * cols
    part = jax.ShapeDtypeStruct((rhs, wide), F32)
    down_call = vmem_call(down_body, (part, part), "down_product", flops)
    turned_call = vmem_call(turned_body, (part, part), "turned_product", flops)
    up_call = vmem_call(up_body, jax.ShapeDtypeStruct((chips, rhs, wide), BF16), "up_product", flops)

    def ordered(x, other, first_on_0):
        halves = [jnp.where(on_0, x, other), jnp.where(on_0, other, x)]
        return jnp.concatenate(halves if first_on_0 else halves[::-1], axis=1).astype(BF16)

    def up_product(full, mat, base, *beside):
        blocks = up_call(full, mat)
        if beside:
            blocks, base, *beside = tie(blocks, base, *beside)
        x = base + jnp.sum(exchange(blocks).astype(F32), axis=0)
        return (x, base, *beside) if beside else x

    down_own, up_own = down_source.reshape(rhs, rows), up_source.reshape(rhs, rows)
    half = chips // 2
    sent_0, matrix, down_own, up_own = tie(second_halves(matrix, 0, half, chips), matrix, down_own, up_own)
    down_got, up_other, received_0 = swap(down_own[:, :wide]), swap(up_own), swap(sent_0)
    sent_1, down_got, up_other = tie(second_halves(matrix, half, chips - half, chips), down_got, up_other)
    received = (received_0, swap(sent_1))
    up_a = jnp.where(on_0, up_own[:, :wide], up_other[:, wide:])
    up_b = jnp.where(on_0, up_other[:, wide:], up_own[:, :wide])
    up_b_rest = jnp.where(on_0, up_other[:, :wide], up_own[:, wide:])
    base_a = jnp.where(on_0, down_own[:, wide:], down_got)
    base_b = jnp.where(on_0, down_got, down_own[:, wide:])
    down_a, down_b = base_a, base_b

    x, base_b, up_a, up_b, up_b_rest, me, tile_0, tile_1, on_0, masks = tie(
        base_a, base_b, up_a, up_b, up_b_rest, me, tile_0, tile_1, on_0, masks
    )
    late = 4
    for p in range(planes):
        if p > 0:
            blocks = spread(hop(x.astype(BF16), p - 1, p))
            if p == 1:
                mine, theirs, matrix_a = load_product(
                    me, 0, late, matrix, received, blocks, tile_1, base_a
                )
            else:
                mine, theirs = turned_call(blocks, matrix_a, tile_1, base_a)
            x = mine + swap(theirs)
            down_a = jnp.where(masks[p], x, down_a)
        blocks = spread(x)
        if p == 0:
            mine, theirs, matrix_b = load_product(me, 1, late, matrix, received, blocks, tile_0, base_b)
        elif p == 1:
            mine, theirs = down_call(blocks, matrix_b, tile_0, base_b)
        else:
            mine, theirs = turned_call(blocks, matrix_b, tile_0, base_b)
        if p == planes - 1:
            break
        x = mine + swap(theirs)
        down_b = jnp.where(masks[p], x, down_b)

    mine, theirs, down_a, down_b = tie(mine, theirs, down_a, down_b)
    rest = up_b_rest + (mine + swap(theirs))
    x = up_b + (theirs + swap(mine))
    x, rest, down_a, down_b = tie(x, rest, down_a, down_b)
    base_b = up_b + swap(down_b)
    base_a = up_a + swap(down_a)
    last_b = x
    full = ordered(x, rest, False)
    for p in reversed(range(planes)):
        if p < planes - 1:
            x = up_product(hop(full, p + 1, p), matrix_b, base_b)
            total_b = jnp.where(masks[p], x, total_b)
            full = ordered(x.astype(BF16), swap(x.astype(BF16)), False)
        if p == planes - 1:
            x, base_a, base_b, last_b = up_product(full, matrix_a, base_a, base_b, last_b)
            total_a, total_b = x, jnp.where(masks[p], last_b, base_b)
        else:
            x = up_product(full, matrix_a, base_a)
            total_a = jnp.where(masks[p], x, total_a)
        if p > 0:
            full = ordered(x.astype(BF16), swap(x.astype(BF16)), True)

    got = swap(jnp.where(on_0, total_b, total_a))
    out = jnp.concatenate([jnp.where(on_0, total_a, total_b), got], axis=1)
    return out.reshape(1, 2, rhs // 2, rows)


def solution(mesh):
    in_specs = (
        P("sweep", None, "layer", None),
        P("sweep", None, None, "layer"),
        P("sweep", None, None, "layer"),
    )
    out_specs = P("sweep", None, None, "layer")
    return jax.shard_map(local, mesh=mesh, in_specs=in_specs, out_specs=out_specs, check_vma=False)
```

```python
import jax
import jax.numpy as jnp
from jax import lax
from jax.experimental import pallas as pl
from jax.experimental.pallas import tpu as pltpu
from jax.sharding import PartitionSpec as P

F32, BF16 = jnp.float32, jnp.bfloat16
MIB = 1 << 20
VMEM = pl.BlockSpec(memory_space=pltpu.VMEM)
HBM = pl.BlockSpec(memory_space=pltpu.HBM)
SMEM = pl.BlockSpec(memory_space=pltpu.SMEM)


def down_sums(x, g, sums):
    contract = (((1,), (1,)), ((), ()))
    r = lax.dot_general(x, g[0], contract, preferred_element_type=F32)
    m = lax.dot_general(x, g[1], contract, preferred_element_type=F32)
    return (r, m) if sums is None else (sums[0] + r, sums[1] + m)


def complex_of(sums, n):
    with_real, with_imag = sums
    return with_real[:n] - with_imag[n:], with_imag[:n] + with_real[n:]


def write_down(sums, base_ref, mine_ref, theirs_ref):
    n, wide = base_ref.shape[0] // 2, base_ref.shape[1]
    real, imag = complex_of(sums, n)
    mine_ref[...] = jnp.concatenate([real[:, :wide], imag[:, :wide]], axis=0) + base_ref[...]
    theirs_ref[...] = jnp.concatenate([real[:, wide:], imag[:, wide:]], axis=0)


def second_halves(matrix, first, count, chips):
    parts, rows, cols = matrix.shape
    wide = cols // (2 * chips)

    def body(matrix_ref, out_ref, held, in_sems, out_sems):
        taken, put = [], []
        for i in range(count):
            at = (2 * (first + i) + 1) * wide
            taken.append(
                pltpu.make_async_copy(matrix_ref.at[:, :, pl.ds(at, wide)], held.at[i], in_sems.at[i])
            )
            put.append(
                pltpu.make_async_copy(held.at[i], out_ref.at[:, :, pl.ds(i * wide, wide)], out_sems.at[i])
            )
        for copy in taken:
            copy.start()
        for i in range(count):
            taken[i].wait()
            put[i].start()
        for copy in put:
            copy.wait()

    return pl.pallas_call(
        body,
        in_specs=[HBM],
        out_specs=HBM,
        out_shape=pltpu.HBM((parts, rows, count * wide), BF16),
        scratch_shapes=[
            pltpu.VMEM((count, parts, rows, wide), BF16),
            pltpu.SemaphoreType.DMA((count,)),
            pltpu.SemaphoreType.DMA((count,)),
        ],
        compiler_params=pltpu.CompilerParams(vmem_limit_bytes=56 * MIB),
        name="second_halves",
    )(matrix)


def load_product(me, on_core, late, matrix, received, blocks, base):
    chips, rhs, wide = blocks.shape
    parts, rows, cols = matrix.shape
    pieces = len(received)

    def body(me_ref, matrix_ref, *refs):
        received_refs = refs[:pieces]
        x_ref, base_ref, mine_ref, theirs_ref, out_ref, sems = refs[pieces:]
        index, per = me_ref[0], chips // pieces

        def copy(source_ref, row, at, i, slot):
            return pltpu.make_async_copy(
                source_ref.at[:, pl.ds(row, wide), pl.ds(at, wide)],
                out_ref.at[pl.ds(0, parts), pl.ds(slot * wide, wide), pl.ds(i * wide, wide)],
                sems.at[slot, i],
            )

        @pl.when(index % 2 == on_core)
        def _():
            for i in range(chips):
                copy(matrix_ref, wide, 2 * i * wide, i, 0).start()
                copy(matrix_ref, 0, 2 * i * wide, i, 1).start()

        @pl.when(index % 2 != on_core)
        def _():
            for i in range(chips):
                copy(received_refs[i // per], 0, i % per * wide, i, 0).start()
                copy(received_refs[i // per], wide, i % per * wide, i, 1).start()

        def wait(i):
            for slot in range(2):
                copy(matrix_ref, 0, 0, i, slot).wait()

        @pl.when(index < late)
        def _():
            sums = None
            for i in range(chips):
                wait(i)
                sums = down_sums(x_ref[i], out_ref.at[:, :, pl.ds(i * wide, wide)], sums)
            write_down(sums, base_ref, mine_ref, theirs_ref)

        @pl.when(index >= late)
        def _():
            for i in range(chips):
                wait(i)
                at = slice(i * wide, (i + 1) * wide)
                for part in range(parts):
                    turned = out_ref[part, :, at].T
                    out_ref[parts + part, :wide, at] = turned[:, :wide]
                    out_ref[parts + part, wide:, at] = turned[:, wide:]
            mine_ref[...] = base_ref[...]
            theirs_ref[...] = base_ref[...]

    part = jax.ShapeDtypeStruct((rhs, wide), F32)
    return pl.pallas_call(
        body,
        in_specs=[SMEM, HBM, *[HBM] * pieces, VMEM, VMEM],
        out_specs=[VMEM] * 3,
        out_shape=[part, part, pltpu.VMEM((2 * parts, rows, cols // 2), BF16)],
        scratch_shapes=[pltpu.SemaphoreType.DMA((2, chips))],
        compiler_params=pltpu.CompilerParams(vmem_limit_bytes=(16 if on_core == 0 else 32) * MIB),
        cost_estimate=pl.CostEstimate(
            flops=4 * rhs * rows * cols, bytes_accessed=parts * rows * cols, transcendentals=0
        ),
        name="load_product",
    )(me, matrix, *received, blocks, base)


def vmem_call(body, out_shape, name, flops):
    def call(*args):
        return pl.pallas_call(
            body,
            in_specs=[VMEM] * len(args),
            out_specs=jax.tree.map(lambda _: VMEM, out_shape),
            out_shape=out_shape,
            compiler_params=pltpu.CompilerParams(vmem_limit_bytes=8 * MIB),
            cost_estimate=pl.CostEstimate(flops=flops, bytes_accessed=1 << 16, transcendentals=0),
            name=name,
        )(*args)

    return call


def down_body(x_ref, g_ref, base_ref, mine_ref, theirs_ref):
    chips, rhs, wide = x_ref.shape
    sums = None
    for i in range(chips):
        sums = down_sums(x_ref[i], g_ref.at[:, :, pl.ds(i * wide, wide)], sums)
    write_down(sums, base_ref, mine_ref, theirs_ref)


def turned_sums(x_ref, g_ref, slot):
    chips, rhs, wide = x_ref.shape
    sums = None
    for i in range(chips):
        terms = [
            jnp.dot(
                x_ref[i],
                g_ref[part, slot * wide : (slot + 1) * wide, i * wide : (i + 1) * wide],
                preferred_element_type=F32,
            )
            for part in (2, 3)
        ]
        sums = terms if sums is None else [total + more for total, more in zip(sums, terms)]
    return jnp.concatenate(complex_of(sums, rhs // 2), axis=0)


def turned_theirs_body(x_ref, g_ref, theirs_ref):
    theirs_ref[...] = turned_sums(x_ref, g_ref, 1)


def turned_mine_body(x_ref, g_ref, base_ref, mine_ref):
    mine_ref[...] = turned_sums(x_ref, g_ref, 0) + base_ref[...]


def up_term(x_ref, g_ref, slot, i):
    rhs, wide = x_ref.shape
    rows, at = slice(slot * wide, (slot + 1) * wide), slice(i * wide, (i + 1) * wide)
    terms = [jnp.dot(x_ref[...], g_ref[part, rows, at], preferred_element_type=F32) for part in range(2)]
    return jnp.concatenate(complex_of(terms, rhs // 2), axis=0)


def up_own_body(x_ref, g_ref, out_ref):
    for i in range(out_ref.shape[0]):
        out_ref[i] = up_term(x_ref, g_ref, 0, i)


def up_rest_body(x_ref, g_ref, own_ref, out_ref):
    for i in range(out_ref.shape[0]):
        out_ref[i] = (up_term(x_ref, g_ref, 1, i) + own_ref[i]).astype(BF16)


def make_masks(me, count, shape):
    def body(me_ref, out_ref):
        index = me_ref[0]
        for p in range(count):
            out_ref[p] = jnp.full(shape, jnp.where(index // 2 == p, 1, 0), jnp.int32)
        out_ref[count] = jnp.full(shape, jnp.where(index % 2 == 0, 1, 0), jnp.int32)

    return pl.pallas_call(
        body,
        in_specs=[SMEM],
        out_specs=VMEM,
        out_shape=pltpu.VMEM((count + 1, *shape), jnp.int32),
        name="make_masks",
    )(me)


def local(green, down_source, up_source):
    planes = lax.axis_size("sweep") // 2
    chips = lax.axis_size("layer")
    matrix = green[0]
    rows, cols = matrix.shape[1:]
    wide = rows // 2
    rhs = 2 * down_source.shape[2]

    def swap(x):
        return lax.ppermute(x, "sweep", [(i, i ^ 1) for i in range(2 * planes)])

    def hop(x, a, b):
        return lax.ppermute(x, "sweep", [(2 * a + c, 2 * b + c) for c in range(2)])

    def hop_across(x, a, b):
        return lax.ppermute(x, "sweep", [(2 * a + c, 2 * b + 1 - c) for c in range(2)])

    def exchange(blocks):
        return lax.all_to_all(blocks, "layer", 0, 0, tiled=True)

    def spread(x):
        return exchange(jnp.broadcast_to(x.astype(BF16), (chips, *x.shape)))

    tie = lambda *values: lax.optimization_barrier(values)
    me = lax.axis_index("sweep").astype(jnp.int32).reshape(1)
    masks = make_masks(me, planes, (rhs, wide))
    masks = [masks[p] == 1 for p in range(planes + 1)]
    on_0 = masks.pop()

    flops = 4 * rhs * rows * cols
    part = jax.ShapeDtypeStruct((rhs, wide), F32)
    down_call = vmem_call(down_body, (part, part), "down_product", flops)
    theirs_call = vmem_call(turned_theirs_body, part, "turned_theirs", flops // 2)
    mine_call = vmem_call(turned_mine_body, part, "turned_mine", flops // 2)
    own_call = vmem_call(up_own_body, jax.ShapeDtypeStruct((chips, rhs, wide), F32), "up_own", flops // 2)
    rest_call = vmem_call(up_rest_body, jax.ShapeDtypeStruct((chips, rhs, wide), BF16), "up_rest", flops // 2)

    def turned_call(blocks, mat, base):
        theirs = theirs_call(blocks, mat)
        return mine_call(blocks, mat, base), theirs

    def up_product(own, other, mat, base, *beside):
        blocks = rest_call(other.astype(BF16), mat, own_call(own.astype(BF16), mat))
        if beside:
            blocks, base, *beside = tie(blocks, base, *beside)
        x = base + jnp.sum(exchange(blocks).astype(F32), axis=0)
        return (x, base, *beside) if beside else x

    down_own, up_own = down_source.reshape(rhs, rows), up_source.reshape(rhs, rows)
    half = chips // 2
    sent_0, matrix, down_own, up_own = tie(second_halves(matrix, 0, half, chips), matrix, down_own, up_own)
    down_got, up_other, received_0 = swap(down_own[:, :wide]), swap(up_own), swap(sent_0)
    sent_1, down_got, up_other = tie(second_halves(matrix, half, chips - half, chips), down_got, up_other)
    received = (received_0, swap(sent_1))
    up_a = jnp.where(on_0, up_own[:, :wide], up_other[:, wide:])
    up_b = jnp.where(on_0, up_other[:, wide:], up_own[:, :wide])
    up_b_rest = jnp.where(on_0, up_other[:, :wide], up_own[:, wide:])
    base_a = jnp.where(on_0, down_own[:, wide:], down_got)
    base_b = jnp.where(on_0, down_got, down_own[:, wide:])
    down_a, mine_b, theirs_b = base_a, base_b, base_b

    x, base_b, up_a, up_b, up_b_rest, me, on_0, masks = tie(
        base_a, base_b, up_a, up_b, up_b_rest, me, on_0, masks
    )
    late = 4
    for p in range(planes):
        if p > 0:
            blocks = spread(hop(mine, p - 1, p) + hop_across(theirs, p - 1, p))
            if p == 1:
                mine, theirs, matrix_a = load_product(
                    me, 0, late, matrix, received, blocks, base_a
                )
            else:
                mine, theirs = turned_call(blocks, matrix_a, base_a)
            x = mine + swap(theirs)
            down_a = jnp.where(masks[p], x, down_a)
        blocks = spread(x)
        if p == 0:
            mine, theirs, matrix_b = load_product(me, 1, late, matrix, received, blocks, base_b)
        elif p == 1:
            mine, theirs = down_call(blocks, matrix_b, base_b)
        else:
            mine, theirs = turned_call(blocks, matrix_b, base_b)
        mine_b = jnp.where(masks[p], mine, mine_b)
        theirs_b = jnp.where(masks[p], theirs, theirs_b)

    mine_b, theirs_b, down_a = tie(mine_b, theirs_b, down_a)
    rest = up_b_rest + (mine_b + swap(theirs_b))
    base_b = up_b + (theirs_b + swap(mine_b))
    base_b, rest, down_a = tie(base_b, rest, down_a)
    base_a = up_a + swap(down_a)
    for p in reversed(range(planes)):
        if p == planes - 1:
            x, base_a, total_b = up_product(base_b, rest, matrix_a, base_a, base_b)
            total_a = x
        else:
            x = x.astype(BF16)
            x = up_product(hop(x, p + 1, p), hop_across(x, p + 1, p), matrix_b, base_b)
            total_b = jnp.where(masks[p], x, total_b)
            x = x.astype(BF16)
            x = up_product(x, swap(x), matrix_a, base_a)
            total_a = jnp.where(masks[p], x, total_a)

    got = swap(jnp.where(on_0, total_b, total_a))
    out = jnp.concatenate([jnp.where(on_0, total_a, total_b), got], axis=1)
    return out.reshape(1, 2, rhs // 2, rows)


def solution(mesh):
    in_specs = (
        P("sweep", None, "layer", None),
        P("sweep", None, None, "layer"),
        P("sweep", None, None, "layer"),
    )
    out_specs = P("sweep", None, None, "layer")
    return jax.shard_map(local, mesh=mesh, in_specs=in_specs, out_specs=out_specs, check_vma=False)
```

```python
import jax
import jax.numpy as jnp
from jax import lax
from jax.experimental import pallas as pl
from jax.experimental.pallas import tpu as pltpu
from jax.sharding import PartitionSpec as P

F32, BF16 = jnp.float32, jnp.bfloat16
MIB = 1 << 20
VMEM = pl.BlockSpec(memory_space=pltpu.VMEM)
HBM = pl.BlockSpec(memory_space=pltpu.HBM)
SMEM = pl.BlockSpec(memory_space=pltpu.SMEM)


def down_sums(x, g, sums):
    contract = (((1,), (1,)), ((), ()))
    r = lax.dot_general(x, g[0], contract, preferred_element_type=F32)
    m = lax.dot_general(x, g[1], contract, preferred_element_type=F32)
    return (r, m) if sums is None else (sums[0] + r, sums[1] + m)


def complex_of(sums, n):
    with_real, with_imag = sums
    return with_real[:n] - with_imag[n:], with_imag[:n] + with_real[n:]


def write_down(sums, base_ref, mine_ref, theirs_ref):
    n, wide = base_ref.shape[0] // 2, base_ref.shape[1]
    real, imag = complex_of(sums, n)
    mine_ref[...] = jnp.concatenate([real[:, :wide], imag[:, :wide]], axis=0) + base_ref[...]
    theirs_ref[...] = jnp.concatenate([real[:, wide:], imag[:, wide:]], axis=0)


def second_halves(matrix, first, count, chips):
    parts, rows, cols = matrix.shape
    wide = cols // (2 * chips)

    def body(matrix_ref, out_ref, held, in_sems, out_sems):
        taken, put = [], []
        for i in range(count):
            at = (2 * (first + i) + 1) * wide
            taken.append(
                pltpu.make_async_copy(matrix_ref.at[:, :, pl.ds(at, wide)], held.at[i], in_sems.at[i])
            )
            put.append(
                pltpu.make_async_copy(held.at[i], out_ref.at[:, :, pl.ds(i * wide, wide)], out_sems.at[i])
            )
        for copy in taken:
            copy.start()
        for i in range(count):
            taken[i].wait()
            put[i].start()
        for copy in put:
            copy.wait()

    return pl.pallas_call(
        body,
        in_specs=[HBM],
        out_specs=HBM,
        out_shape=pltpu.HBM((parts, rows, count * wide), BF16),
        scratch_shapes=[
            pltpu.VMEM((count, parts, rows, wide), BF16),
            pltpu.SemaphoreType.DMA((count,)),
            pltpu.SemaphoreType.DMA((count,)),
        ],
        compiler_params=pltpu.CompilerParams(vmem_limit_bytes=56 * MIB),
        name="second_halves",
    )(matrix)


def load_product(me, on_core, late, matrix, received, blocks, base):
    chips, rhs, wide = blocks.shape
    parts, rows, cols = matrix.shape
    pieces = len(received)

    def body(me_ref, matrix_ref, *refs):
        received_refs = refs[:pieces]
        x_ref, base_ref, mine_ref, theirs_ref, out_ref, sems = refs[pieces:]
        index, per = me_ref[0], chips // pieces

        def copy(source_ref, row, at, i, slot):
            return pltpu.make_async_copy(
                source_ref.at[:, pl.ds(row, wide), pl.ds(at, wide)],
                out_ref.at[pl.ds(0, parts), pl.ds(slot * wide, wide), pl.ds(i * wide, wide)],
                sems.at[slot, i],
            )

        @pl.when(index % 2 == on_core)
        def _():
            for i in range(chips):
                copy(matrix_ref, wide, 2 * i * wide, i, 0).start()
                copy(matrix_ref, 0, 2 * i * wide, i, 1).start()

        @pl.when(index % 2 != on_core)
        def _():
            for i in range(chips):
                copy(received_refs[i // per], 0, i % per * wide, i, 0).start()
                copy(received_refs[i // per], wide, i % per * wide, i, 1).start()

        def wait(i):
            for slot in range(2):
                copy(matrix_ref, 0, 0, i, slot).wait()

        @pl.when(index < late)
        def _():
            sums = None
            for i in range(chips):
                wait(i)
                sums = down_sums(x_ref[i], out_ref.at[:, :, pl.ds(i * wide, wide)], sums)
            write_down(sums, base_ref, mine_ref, theirs_ref)

        @pl.when(index >= late)
        def _():
            for i in range(chips):
                wait(i)
                at = slice(i * wide, (i + 1) * wide)
                for part in range(parts):
                    turned = out_ref[part, :, at].T
                    out_ref[parts + part, :wide, at] = turned[:, :wide]
                    out_ref[parts + part, wide:, at] = turned[:, wide:]
            mine_ref[...] = base_ref[...]
            theirs_ref[...] = base_ref[...]

    part = jax.ShapeDtypeStruct((rhs, wide), F32)
    return pl.pallas_call(
        body,
        in_specs=[SMEM, HBM, *[HBM] * pieces, VMEM, VMEM],
        out_specs=[VMEM] * 3,
        out_shape=[part, part, pltpu.VMEM((2 * parts, rows, cols // 2), BF16)],
        scratch_shapes=[pltpu.SemaphoreType.DMA((2, chips))],
        compiler_params=pltpu.CompilerParams(vmem_limit_bytes=(16 if on_core == 0 else 32) * MIB),
        cost_estimate=pl.CostEstimate(
            flops=4 * rhs * rows * cols, bytes_accessed=parts * rows * cols, transcendentals=0
        ),
        name="load_product",
    )(me, matrix, *received, blocks, base)


def vmem_call(body, out_shape, name, flops):
    def call(*args):
        return pl.pallas_call(
            body,
            in_specs=[VMEM] * len(args),
            out_specs=jax.tree.map(lambda _: VMEM, out_shape),
            out_shape=out_shape,
            compiler_params=pltpu.CompilerParams(vmem_limit_bytes=8 * MIB),
            cost_estimate=pl.CostEstimate(flops=flops, bytes_accessed=1 << 16, transcendentals=0),
            name=name,
        )(*args)

    return call


def rows_sums(x_ref, g_ref, slot):
    chips, rhs, wide = x_ref.shape
    sums = None
    for i in range(chips):
        part_ref = g_ref.at[:, pl.ds(slot * wide, wide), pl.ds(i * wide, wide)]
        sums = down_sums(x_ref[i], part_ref, sums)
    return jnp.concatenate(complex_of(sums, rhs // 2), axis=0)


def rows_theirs_body(x_ref, g_ref, theirs_ref):
    theirs_ref[...] = rows_sums(x_ref, g_ref, 1)


def rows_mine_body(x_ref, g_ref, base_ref, mine_ref):
    mine_ref[...] = rows_sums(x_ref, g_ref, 0) + base_ref[...]


def turned_sums(x_ref, g_ref, slot):
    chips, rhs, wide = x_ref.shape
    sums = None
    for i in range(chips):
        terms = [
            jnp.dot(
                x_ref[i],
                g_ref[part, slot * wide : (slot + 1) * wide, i * wide : (i + 1) * wide],
                preferred_element_type=F32,
            )
            for part in (2, 3)
        ]
        sums = terms if sums is None else [total + more for total, more in zip(sums, terms)]
    return jnp.concatenate(complex_of(sums, rhs // 2), axis=0)


def turned_theirs_body(x_ref, g_ref, theirs_ref):
    theirs_ref[...] = turned_sums(x_ref, g_ref, 1)


def turned_mine_body(x_ref, g_ref, base_ref, mine_ref):
    mine_ref[...] = turned_sums(x_ref, g_ref, 0) + base_ref[...]


def up_term(x_ref, g_ref, slot, i):
    rhs, wide = x_ref.shape
    rows, at = slice(slot * wide, (slot + 1) * wide), slice(i * wide, (i + 1) * wide)
    terms = [jnp.dot(x_ref[...], g_ref[part, rows, at], preferred_element_type=F32) for part in range(2)]
    return jnp.concatenate(complex_of(terms, rhs // 2), axis=0)


def up_own_body(x_ref, g_ref, out_ref):
    for i in range(out_ref.shape[0]):
        out_ref[i] = up_term(x_ref, g_ref, 0, i)


def up_rest_body(x_ref, g_ref, own_ref, out_ref):
    for i in range(out_ref.shape[0]):
        out_ref[i] = (up_term(x_ref, g_ref, 1, i) + own_ref[i]).astype(BF16)


def make_masks(me, count, shape):
    def body(me_ref, out_ref):
        index = me_ref[0]
        for p in range(count):
            out_ref[p] = jnp.full(shape, jnp.where(index // 2 == p, 1, 0), jnp.int32)
        out_ref[count] = jnp.full(shape, jnp.where(index % 2 == 0, 1, 0), jnp.int32)

    return pl.pallas_call(
        body,
        in_specs=[SMEM],
        out_specs=VMEM,
        out_shape=pltpu.VMEM((count + 1, *shape), jnp.int32),
        name="make_masks",
    )(me)


def local(green, down_source, up_source):
    planes = lax.axis_size("sweep") // 2
    chips = lax.axis_size("layer")
    matrix = green[0]
    rows, cols = matrix.shape[1:]
    wide = rows // 2
    rhs = 2 * down_source.shape[2]

    def swap(x):
        return lax.ppermute(x, "sweep", [(i, i ^ 1) for i in range(2 * planes)])

    def hop(x, a, b):
        return lax.ppermute(x, "sweep", [(2 * a + c, 2 * b + c) for c in range(2)])

    def hop_across(x, a, b):
        return lax.ppermute(x, "sweep", [(2 * a + c, 2 * b + 1 - c) for c in range(2)])

    def exchange(blocks):
        return lax.all_to_all(blocks, "layer", 0, 0, tiled=True)

    def spread(x):
        return exchange(jnp.broadcast_to(x.astype(BF16), (chips, *x.shape)))

    tie = lambda *values: lax.optimization_barrier(values)
    me = lax.axis_index("sweep").astype(jnp.int32).reshape(1)
    masks = make_masks(me, planes, (rhs, wide))
    masks = [masks[p] == 1 for p in range(planes + 1)]
    on_0 = masks.pop()

    flops = 4 * rhs * rows * cols
    part = jax.ShapeDtypeStruct((rhs, wide), F32)
    rows_theirs = vmem_call(rows_theirs_body, part, "rows_theirs", flops // 2)
    rows_mine = vmem_call(rows_mine_body, part, "rows_mine", flops // 2)
    theirs_call = vmem_call(turned_theirs_body, part, "turned_theirs", flops // 2)
    mine_call = vmem_call(turned_mine_body, part, "turned_mine", flops // 2)
    own_call = vmem_call(up_own_body, jax.ShapeDtypeStruct((chips, rhs, wide), F32), "up_own", flops // 2)
    rest_call = vmem_call(up_rest_body, jax.ShapeDtypeStruct((chips, rhs, wide), BF16), "up_rest", flops // 2)

    def turned_call(blocks, mat, base):
        theirs = theirs_call(blocks, mat)
        return mine_call(blocks, mat, base), theirs

    def up_product(own, other, mat, base, *beside):
        blocks = rest_call(other.astype(BF16), mat, own_call(own.astype(BF16), mat))
        if beside:
            blocks, base, *beside = tie(blocks, base, *beside)
        x = base + jnp.sum(exchange(blocks).astype(F32), axis=0)
        return (x, base, *beside) if beside else x

    down_own, up_own = down_source.reshape(rhs, rows), up_source.reshape(rhs, rows)
    half = chips // 2
    sent_0, matrix, down_own, up_own = tie(second_halves(matrix, 0, half, chips), matrix, down_own, up_own)
    down_got, up_other, received_0 = swap(down_own[:, :wide]), swap(up_own), swap(sent_0)
    sent_1, down_got, up_other = tie(second_halves(matrix, half, chips - half, chips), down_got, up_other)
    received = (received_0, swap(sent_1))
    up_a = jnp.where(on_0, up_own[:, :wide], up_other[:, wide:])
    up_b = jnp.where(on_0, up_other[:, wide:], up_own[:, :wide])
    up_b_rest = jnp.where(on_0, up_other[:, :wide], up_own[:, wide:])
    base_a = jnp.where(on_0, down_own[:, wide:], down_got)
    base_b = jnp.where(on_0, down_got, down_own[:, wide:])
    down_a, mine_b, theirs_b = base_a, base_b, base_b

    x, base_b, up_a, up_b, up_b_rest, me, on_0, masks = tie(
        base_a, base_b, up_a, up_b, up_b_rest, me, on_0, masks
    )
    late = 4
    for p in range(planes):
        if p > 0:
            blocks = spread(hop(mine, p - 1, p) + hop_across(theirs, p - 1, p))
            if p == 1:
                mine, theirs, matrix_a = load_product(
                    me, 0, late, matrix, received, blocks, base_a
                )
            else:
                mine, theirs = turned_call(blocks, matrix_a, base_a)
            x = mine + swap(theirs)
            down_a = jnp.where(masks[p], x, down_a)
        blocks = spread(x)
        if p == 0:
            mine, theirs, matrix_b = load_product(me, 1, late, matrix, received, blocks, base_b)
        elif p == 1:
            theirs, mine = rows_theirs(blocks, matrix_b), rows_mine(blocks, matrix_b, base_b)
        else:
            mine, theirs = turned_call(blocks, matrix_b, base_b)
        mine_b = jnp.where(masks[p], mine, mine_b)
        theirs_b = jnp.where(masks[p], theirs, theirs_b)

    mine_b, theirs_b, down_a = tie(mine_b, theirs_b, down_a)
    rest = up_b_rest + (mine_b + swap(theirs_b))
    base_b = up_b + (theirs_b + swap(mine_b))
    base_b, rest, down_a = tie(base_b, rest, down_a)
    base_a = up_a + swap(down_a)
    for p in reversed(range(planes)):
        if p == planes - 1:
            x, base_a, total_b = up_product(base_b, rest, matrix_a, base_a, base_b)
            total_a = x
        else:
            x = x.astype(BF16)
            x = up_product(hop(x, p + 1, p), hop_across(x, p + 1, p), matrix_b, base_b)
            total_b = jnp.where(masks[p], x, total_b)
            x = x.astype(BF16)
            x = up_product(x, swap(x), matrix_a, base_a)
            total_a = jnp.where(masks[p], x, total_a)

    got = swap(jnp.where(on_0, total_b, total_a))
    out = jnp.concatenate([jnp.where(on_0, total_a, total_b), got], axis=1)
    return out.reshape(1, 2, rhs // 2, rows)


def solution(mesh):
    in_specs = (
        P("sweep", None, "layer", None),
        P("sweep", None, None, "layer"),
        P("sweep", None, None, "layer"),
    )
    out_specs = P("sweep", None, None, "layer")
    return jax.shard_map(local, mesh=mesh, in_specs=in_specs, out_specs=out_specs, check_vma=False)
```

```python
import jax
import jax.numpy as jnp
from jax import lax
from jax.experimental import pallas as pl
from jax.experimental.pallas import tpu as pltpu
from jax.sharding import PartitionSpec as P

F32, BF16 = jnp.float32, jnp.bfloat16
MIB = 1 << 20
VMEM = pl.BlockSpec(memory_space=pltpu.VMEM)
HBM = pl.BlockSpec(memory_space=pltpu.HBM)
SMEM = pl.BlockSpec(memory_space=pltpu.SMEM)


def down_sums(x, g, sums):
    contract = (((1,), (1,)), ((), ()))
    r = lax.dot_general(x, g[0], contract, preferred_element_type=F32)
    m = lax.dot_general(x, g[1], contract, preferred_element_type=F32)
    return (r, m) if sums is None else (sums[0] + r, sums[1] + m)


def complex_of(sums, n):
    with_real, with_imag = sums
    return with_real[:n] - with_imag[n:], with_imag[:n] + with_real[n:]


def write_down(sums, base_ref, mine_ref, theirs_ref):
    n, wide = base_ref.shape[0] // 2, base_ref.shape[1]
    real, imag = complex_of(sums, n)
    mine_ref[...] = jnp.concatenate([real[:, :wide], imag[:, :wide]], axis=0) + base_ref[...]
    theirs_ref[...] = jnp.concatenate([real[:, wide:], imag[:, wide:]], axis=0)


def second_halves(matrix, first, count, chips):
    parts, rows, cols = matrix.shape
    wide = cols // (2 * chips)

    def body(matrix_ref, out_ref, held, in_sems, out_sems):
        taken, put = [], []
        for i in range(count):
            at = (2 * (first + i) + 1) * wide
            taken.append(
                pltpu.make_async_copy(matrix_ref.at[:, :, pl.ds(at, wide)], held.at[i], in_sems.at[i])
            )
            put.append(
                pltpu.make_async_copy(held.at[i], out_ref.at[:, :, pl.ds(i * wide, wide)], out_sems.at[i])
            )
        for copy in taken:
            copy.start()
        for i in range(count):
            taken[i].wait()
            put[i].start()
        for copy in put:
            copy.wait()

    return pl.pallas_call(
        body,
        in_specs=[HBM],
        out_specs=HBM,
        out_shape=pltpu.HBM((parts, rows, count * wide), BF16),
        scratch_shapes=[
            pltpu.VMEM((count, parts, rows, wide), BF16),
            pltpu.SemaphoreType.DMA((count,)),
            pltpu.SemaphoreType.DMA((count,)),
        ],
        compiler_params=pltpu.CompilerParams(vmem_limit_bytes=56 * MIB),
        name="second_halves",
    )(matrix)


def load_product(me, on_core, late, matrix, received, blocks, base):
    chips, rhs, wide = blocks.shape
    parts, rows, cols = matrix.shape
    pieces = len(received)

    def body(me_ref, matrix_ref, *refs):
        received_refs = refs[:pieces]
        x_ref, base_ref, mine_ref, theirs_ref, out_ref, sems = refs[pieces:]
        index, per = me_ref[0], chips // pieces

        def copy(source_ref, row, at, i, slot):
            return pltpu.make_async_copy(
                source_ref.at[:, pl.ds(row, wide), pl.ds(at, wide)],
                out_ref.at[pl.ds(0, parts), pl.ds(slot * wide, wide), pl.ds(i * wide, wide)],
                sems.at[slot, i],
            )

        @pl.when(index % 2 == on_core)
        def _():
            for i in range(chips):
                copy(matrix_ref, wide, 2 * i * wide, i, 0).start()
                copy(matrix_ref, 0, 2 * i * wide, i, 1).start()

        @pl.when(index % 2 != on_core)
        def _():
            for i in range(chips):
                copy(received_refs[i // per], 0, i % per * wide, i, 0).start()
                copy(received_refs[i // per], wide, i % per * wide, i, 1).start()

        def wait(i):
            for slot in range(2):
                copy(matrix_ref, 0, 0, i, slot).wait()

        @pl.when(index < late)
        def _():
            sums = None
            for i in range(chips):
                wait(i)
                sums = down_sums(x_ref[i], out_ref.at[:, :, pl.ds(i * wide, wide)], sums)
            write_down(sums, base_ref, mine_ref, theirs_ref)

        @pl.when(index >= late)
        def _():
            for i in range(chips):
                wait(i)
                at = slice(i * wide, (i + 1) * wide)
                for part in range(parts):
                    turned = out_ref[part, :, at].T
                    out_ref[parts + part, :wide, at] = turned[:, :wide]
                    out_ref[parts + part, wide:, at] = turned[:, wide:]
            mine_ref[...] = base_ref[...]
            theirs_ref[...] = base_ref[...]

    part = jax.ShapeDtypeStruct((rhs, wide), F32)
    return pl.pallas_call(
        body,
        in_specs=[SMEM, HBM, *[HBM] * pieces, VMEM, VMEM],
        out_specs=[VMEM] * 3,
        out_shape=[part, part, pltpu.VMEM((2 * parts, rows, cols // 2), BF16)],
        scratch_shapes=[pltpu.SemaphoreType.DMA((2, chips))],
        compiler_params=pltpu.CompilerParams(vmem_limit_bytes=(16 if on_core == 0 else 32) * MIB),
        cost_estimate=pl.CostEstimate(
            flops=4 * rhs * rows * cols, bytes_accessed=parts * rows * cols, transcendentals=0
        ),
        name="load_product",
    )(me, matrix, *received, blocks, base)


def vmem_call(body, out_shape, name, flops):
    def call(*args):
        return pl.pallas_call(
            body,
            in_specs=[VMEM] * len(args),
            out_specs=jax.tree.map(lambda _: VMEM, out_shape),
            out_shape=out_shape,
            compiler_params=pltpu.CompilerParams(vmem_limit_bytes=8 * MIB),
            cost_estimate=pl.CostEstimate(flops=flops, bytes_accessed=1 << 16, transcendentals=0),
            name=name,
        )(*args)

    return call


def down_body(x_ref, g_ref, base_ref, mine_ref, theirs_ref):
    chips, rhs, wide = x_ref.shape
    sums = None
    for i in range(chips):
        sums = down_sums(x_ref[i], g_ref.at[:, :, pl.ds(i * wide, wide)], sums)
    write_down(sums, base_ref, mine_ref, theirs_ref)


def turned_sums(x_ref, g_ref, slot):
    chips, rhs, wide = x_ref.shape
    sums = None
    for i in range(chips):
        terms = [
            jnp.dot(
                x_ref[i],
                g_ref[part, slot * wide : (slot + 1) * wide, i * wide : (i + 1) * wide],
                preferred_element_type=F32,
            )
            for part in (2, 3)
        ]
        sums = terms if sums is None else [total + more for total, more in zip(sums, terms)]
    return jnp.concatenate(complex_of(sums, rhs // 2), axis=0)


def turned_theirs_body(x_ref, g_ref, theirs_ref):
    theirs_ref[...] = turned_sums(x_ref, g_ref, 1)


def turned_mine_body(x_ref, g_ref, base_ref, mine_ref):
    mine_ref[...] = turned_sums(x_ref, g_ref, 0) + base_ref[...]


def up_term(x_ref, g_ref, slot, i):
    rhs, wide = x_ref.shape
    rows, at = slice(slot * wide, (slot + 1) * wide), slice(i * wide, (i + 1) * wide)
    terms = [jnp.dot(x_ref[...], g_ref[part, rows, at], preferred_element_type=F32) for part in range(2)]
    return jnp.concatenate(complex_of(terms, rhs // 2), axis=0)


def up_own_body(x_ref, g_ref, out_ref):
    for i in range(out_ref.shape[0]):
        out_ref[i] = up_term(x_ref, g_ref, 0, i)


def up_rest_body(x_ref, g_ref, own_ref, out_ref):
    for i in range(out_ref.shape[0]):
        out_ref[i] = (up_term(x_ref, g_ref, 1, i) + own_ref[i]).astype(BF16)


def make_masks(me, count, shape):
    def body(me_ref, out_ref):
        index = me_ref[0]
        for p in range(count):
            out_ref[p] = jnp.full(shape, jnp.where(index // 2 == p, 1, 0), jnp.int32)
        out_ref[count] = jnp.full(shape, jnp.where(index % 2 == 0, 1, 0), jnp.int32)

    return pl.pallas_call(
        body,
        in_specs=[SMEM],
        out_specs=VMEM,
        out_shape=pltpu.VMEM((count + 1, *shape), jnp.int32),
        name="make_masks",
    )(me)


def local(green, down_source, up_source):
    planes = lax.axis_size("sweep") // 2
    chips = lax.axis_size("layer")
    matrix = green[0]
    rows, cols = matrix.shape[1:]
    wide = rows // 2
    rhs = 2 * down_source.shape[2]

    def swap(x):
        return lax.ppermute(x, "sweep", [(i, i ^ 1) for i in range(2 * planes)])

    def hop(x, a, b):
        return lax.ppermute(x, "sweep", [(2 * a + c, 2 * b + c) for c in range(2)])

    def hop_across(x, a, b):
        return lax.ppermute(x, "sweep", [(2 * a + c, 2 * b + 1 - c) for c in range(2)])

    def exchange(blocks):
        return lax.all_to_all(blocks, "layer", 0, 0, tiled=True)

    def spread(x):
        return exchange(jnp.broadcast_to(x.astype(BF16), (chips, *x.shape)))

    tie = lambda *values: lax.optimization_barrier(values)
    me = lax.axis_index("sweep").astype(jnp.int32).reshape(1)
    masks = make_masks(me, planes, (rhs, wide))
    masks = [masks[p] == 1 for p in range(planes + 1)]
    on_0 = masks.pop()

    flops = 4 * rhs * rows * cols
    part = jax.ShapeDtypeStruct((rhs, wide), F32)
    down_call = vmem_call(down_body, (part, part), "down_product", flops)
    theirs_call = vmem_call(turned_theirs_body, part, "turned_theirs", flops // 2)
    mine_call = vmem_call(turned_mine_body, part, "turned_mine", flops // 2)
    own_call = vmem_call(up_own_body, jax.ShapeDtypeStruct((chips, rhs, wide), F32), "up_own", flops // 2)
    rest_call = vmem_call(up_rest_body, jax.ShapeDtypeStruct((chips, rhs, wide), BF16), "up_rest", flops // 2)

    def turned_call(blocks, mat, base):
        theirs = theirs_call(blocks, mat)
        return mine_call(blocks, mat, base), theirs

    def up_product(own, other, mat, base, *beside):
        blocks = rest_call(other.astype(BF16), mat, own_call(own.astype(BF16), mat))
        if beside:
            blocks, base, *beside = tie(blocks, base, *beside)
        x = base + jnp.sum(exchange(blocks).astype(F32), axis=0)
        return (x, base, *beside) if beside else x

    down_own, up_own = down_source.reshape(rhs, rows), up_source.reshape(rhs, rows)
    half = chips // 2
    sent_0, matrix, down_own, up_own = tie(second_halves(matrix, 0, half, chips), matrix, down_own, up_own)
    down_got, up_other, received_0 = swap(down_own[:, :wide]), swap(up_own), swap(sent_0)
    sent_1, down_got, up_other = tie(second_halves(matrix, half, chips - half, chips), down_got, up_other)
    received = (received_0, swap(sent_1))
    up_a = jnp.where(on_0, up_own[:, :wide], up_other[:, wide:])
    up_b = jnp.where(on_0, up_other[:, wide:], up_own[:, :wide])
    up_b_rest = jnp.where(on_0, up_other[:, :wide], up_own[:, wide:])
    base_a = jnp.where(on_0, down_own[:, wide:], down_got)
    base_b = jnp.where(on_0, down_got, down_own[:, wide:])
    down_a, mine_b, theirs_b = base_a, base_b, base_b

    x, base_b, up_a, up_b, up_b_rest, me, on_0, masks = tie(
        base_a, base_b, up_a, up_b, up_b_rest, me, on_0, masks
    )
    late = 4
    for p in range(planes):
        if p > 0:
            blocks = spread(hop((mine + swap(theirs)).astype(BF16), p - 1, p))
            if p == 1:
                mine, theirs, matrix_a = load_product(
                    me, 0, late, matrix, received, blocks, base_a
                )
            else:
                mine, theirs = turned_call(blocks, matrix_a, base_a)
            x = mine + swap(theirs)
            down_a = jnp.where(masks[p], x, down_a)
        blocks = spread(x)
        if p == 0:
            mine, theirs, matrix_b = load_product(me, 1, late, matrix, received, blocks, base_b)
        elif p == 1:
            mine, theirs = down_call(blocks, matrix_b, base_b)
        else:
            mine, theirs = turned_call(blocks, matrix_b, base_b)
        mine_b = jnp.where(masks[p], mine, mine_b)
        theirs_b = jnp.where(masks[p], theirs, theirs_b)

    mine_b, theirs_b, down_a = tie(mine_b, theirs_b, down_a)
    rest = up_b_rest + (mine_b + swap(theirs_b))
    base_b = up_b + (theirs_b + swap(mine_b))
    base_b, rest, down_a = tie(base_b, rest, down_a)
    base_a = up_a + swap(down_a)
    for p in reversed(range(planes)):
        if p == planes - 1:
            x, base_a, total_b = up_product(base_b, rest, matrix_a, base_a, base_b)
            total_a = x
        else:
            x = x.astype(BF16)
            x = up_product(hop(x, p + 1, p), hop_across(x, p + 1, p), matrix_b, base_b)
            total_b = jnp.where(masks[p], x, total_b)
            x = x.astype(BF16)
            x = up_product(x, swap(x), matrix_a, base_a)
            total_a = jnp.where(masks[p], x, total_a)

    got = swap(jnp.where(on_0, total_b, total_a))
    out = jnp.concatenate([jnp.where(on_0, total_a, total_b), got], axis=1)
    return out.reshape(1, 2, rhs // 2, rows)


def solution(mesh):
    in_specs = (
        P("sweep", None, "layer", None),
        P("sweep", None, None, "layer"),
        P("sweep", None, None, "layer"),
    )
    out_specs = P("sweep", None, None, "layer")
    return jax.shard_map(local, mesh=mesh, in_specs=in_specs, out_specs=out_specs, check_vma=False)
```
